32 devices in a mesh: across: 2 (over y), along: 16 (over z, x, core).
Axes of the slice: x: 2, y: 2, z: 4, core: 2. Of those that a mesh axis runs over, the one named last changes fastest.
Arguments:
- retard: bfloat16 [256, 2048], P('across', 'along'), may hold values from -0.0078125 to 0.0078125
- cotangent: bfloat16 [8, 256, 2048], P(None, 'across', 'along'), may hold values from -6 to 6
- filters: bfloat16 [8, 128, 128], replicated, may hold values from -0.015625 to 0.015625
Outputs:
- grad_input: float32 [256, 2048], P('across', 'along')
- grad_filters: float32 [8, 128, 128], replicated
The draws below stay inside these ranges and needn't reach their ends.
All inputs are finite; a program needn't handle non-finite values.
Results may differ from the reference program's by a relative error of at most 0.0003.
Values may be sent and summed in bfloat16 or wider, within the bound.
No kernel may reach another device: no remote copies, remote signals or barrier semaphores. Data moves between devices by JAX's collectives and lax.ppermute only.
A program may use at most 64 MiB of HBM per device.

```python
import jax
import jax.numpy as jnp
from jax import lax

F = 8
R = 128
ROWS = 256
COLS = 2048


def block_levels(stream_key, dims, pieces, low, high):
    gain = 1.0
    for position, parts in pieces:
        heights = jax.random.uniform(jax.random.fold_in(jax.random.fold_in(stream_key, 6), position), (parts,), jnp.float32, low / len(pieces), high / len(pieces))
        gain = gain * jnp.repeat(jnp.exp(heights), dims[position] // parts).reshape((-1,) + (1,) * (len(dims) - 1 - position))
    return gain


def bell_draw(key, extent, width, limit, split=(), held_as=jnp.bfloat16):
    result = width * jax.random.normal(key, extent, jnp.float32)
    if split:
        result = result * block_levels(key, extent, split, -0.22, 0.18)
    return jnp.clip(result, -limit, limit).astype(held_as)


def setup_inputs(seed: int = 0) -> dict:
    seeds = jax.random.split(jax.random.key(seed), 4)
    return {
        "retard": bell_draw(seeds[0], (ROWS, COLS), (ROWS * COLS) ** -0.5, 0.0078125, ((0, 2), (1, 16))),
        "cotangent": bell_draw(seeds[1], (F, ROWS, COLS), 1.0, 6.0, ((1, 2), (2, 16))),
        "filters": bell_draw(seeds[2], (F, R, R), (F * R * R) ** -0.5, 0.015625),
    }


def reference(retard, cotangent, filters):
    radius = filters.shape[1]
    margin = radius // 2
    rows_total, cols_total = retard.shape
    shape_fft = (rows_total + radius, cols_total + radius)
    retard_map = retard.astype(jnp.float32)
    retard_spec = jnp.fft.rfft2(jnp.pad(retard_map, ((margin, 0), (margin, 0))), s=shape_fft)

    def per_filter(operands):
        grad_map, kernel = operands
        grad_spec = jnp.fft.rfft2(grad_map.astype(jnp.float32), s=shape_fft)
        kernel_spec = jnp.fft.rfft2(kernel.astype(jnp.float32), s=shape_fft)
        full_conv = jnp.fft.irfft2(grad_spec * kernel_spec, s=shape_fft)
        input_part = full_conv[margin:margin + rows_total, margin:margin + cols_total]
        matched = jnp.fft.irfft2(jnp.conj(grad_spec) * retard_spec, s=shape_fft)[:radius, :radius]
        return input_part.astype(jnp.float32), matched.astype(jnp.float32)

    input_parts, grad_filters = lax.map(per_filter, (cotangent, filters))
    return jnp.sum(input_parts, axis=0), grad_filters
```

```python
import functools
import math

import jax
import jax.numpy as jnp
import numpy as np
from jax import lax
from jax.experimental import pallas as pl
from jax.experimental.pallas import tpu as pltpu
from jax.sharding import PartitionSpec as P

AXES = ("across", "along")
f32 = jnp.float32
bf16 = jnp.bfloat16


def halves(table):
    upper = table.astype(np.float32).astype(jnp.bfloat16)
    lower = (table - upper.astype(np.float64)).astype(np.float32).astype(jnp.bfloat16)
    return upper, lower


def tables(radius):
    period = 2 * radius
    freq = np.arange(radius)[:, None] + 0.5

    def turn(position):
        angle = 2.0 * math.pi / period * freq * position[None, :]
        return np.cos(angle), np.sin(angle)

    near = np.arange(radius)
    wide = (np.arange(period) + radius // 2) % period
    out = {}
    cos_n, sin_n = turn(near)
    cos_w, sin_w = turn(wide)
    hi, lo = halves(np.concatenate([cos_n, sin_n], axis=0))
    out["rows_near"] = np.concatenate([hi, lo], axis=1)
    hi, lo = halves(np.concatenate([cos_n, -sin_n], axis=0).T)
    out["cols_near"] = np.concatenate([hi, hi, lo], axis=0)
    hi, lo = halves(np.concatenate([cos_w, sin_w], axis=0))
    out["rows_wide"] = np.concatenate([hi, lo], axis=1)
    hi, lo = halves(np.concatenate([cos_w, -sin_w], axis=0).T)
    out["cols_wide"] = np.concatenate([hi, hi, lo], axis=0)
    scale = 2.0 / period**2
    hi, lo = halves(np.concatenate([cos_n, sin_n], axis=0).T)
    out["back_rows_near"] = np.concatenate([hi, lo], axis=0)
    hi, lo = halves(np.concatenate([cos_n, -sin_n], axis=0) * scale)
    out["back_cols_near"] = np.concatenate([hi, lo], axis=1)
    hi, lo = halves(np.concatenate([cos_w, sin_w], axis=0).T)
    out["back_rows_wide"] = np.concatenate([hi, lo], axis=0)
    hi, lo = halves(np.concatenate([cos_w, -sin_w], axis=0) * scale)
    out["back_cols_wide"] = np.concatenate([hi, lo], axis=1)
    return out


def dot(a, b):
    return jnp.dot(a, b, preferred_element_type=f32)


def split(x):
    upper = x.astype(bf16)
    return upper, (x - upper.astype(f32)).astype(bf16)


def butterfly(mixed, radius):
    cr, ci = mixed[:radius, :radius], mixed[:radius, radius:]
    sr, si = mixed[radius:, :radius], mixed[radius:, radius:]
    return (cr + si, ci - sr), (cr - si, ci + sr)


def near_spectra(first, second, rows, cols, radius):
    pair = jnp.concatenate([first, second], axis=1)
    mixed = dot(rows, jnp.concatenate([pair, pair], axis=0))
    result = []
    for part in (mixed[:, :radius], mixed[:, radius:]):
        hi, lo = split(part)
        result.append(butterfly(dot(jnp.concatenate([hi, lo, hi], axis=1), cols), radius))
    return result


def inverse(plus, minus, rows, cols):
    (pr, pi), (mr, mi) = plus, minus
    mixed = jnp.concatenate(
        [
            jnp.concatenate([pr + mr, pi + mi], axis=1),
            jnp.concatenate([mi - pi, pr - mr], axis=1),
        ],
        axis=0,
    )
    count = rows.shape[0] // 2
    hi, lo = split(mixed)
    both = dot(rows, hi)
    part = both[:count] + both[count:] + dot(rows[:count], lo)
    width = cols.shape[1] // 2
    hi, lo = split(part)
    both = dot(hi, cols)
    return both[:, :width] + both[:, width:] + dot(lo, cols[:, :width])


def cotangent_kernel(cot_ref, rows_ref, cols_ref, out_ref):
    count, radius = cot_ref.shape[0], cot_ref.shape[1]
    for f in range(0, count, 2):
        spectra = near_spectra(cot_ref[f], cot_ref[f + 1], rows_ref[...], cols_ref[...], radius)
        for g, (plus, minus) in enumerate(spectra):
            out_ref[f + g, 0] = plus[0]
            out_ref[f + g, 1] = plus[1]
            out_ref[f + g, 2] = minus[0]
            out_ref[f + g, 3] = minus[1]


def row_pick(shape, start):
    row = lax.broadcasted_iota(jnp.int32, shape, 0)
    return row < shape[0] // 2 if start else row >= shape[0] // 2


def filters_kernel(two, place_ref, spec_ref, own_ref, *rest):
    pieces, (rows_w, cols_w, rows_b, cols_b, keep_ref, send_ref) = rest[:-6], rest[-6:]
    radius = own_ref.shape[0]
    shape = (radius, radius)
    low_row = lax.broadcasted_iota(jnp.int32, shape, 0) < radius // 2
    low_col = lax.broadcasted_iota(jnp.int32, shape, 1) < radius // 2
    zero = jnp.zeros(shape, f32)
    got = [p[...].astype(f32) for p in pieces]
    left, right = got[:2]
    side = jnp.where(low_col, right, left)
    if two:
        mid, diag_left, diag_right = got[2:]
        use = low_row == (place_ref[2] == 0)
        below = jnp.where(use, mid, zero)
        corner = jnp.where(use, jnp.where(low_col, diag_right, diag_left), zero)
    else:
        up, up_left, up_right, down, down_left, down_right = got[2:]
        below = jnp.where(low_row, down, up)
        corner = jnp.where(
            low_row,
            jnp.where(low_col, down_right, down_left),
            jnp.where(low_col, up_right, up_left),
        )
    window = jnp.concatenate(
        [
            jnp.concatenate([own_ref[...], side.astype(bf16)], axis=1),
            jnp.concatenate([below.astype(bf16), corner.astype(bf16)], axis=1),
        ],
        axis=0,
    )
    mixed = dot(rows_w[...], jnp.concatenate([window, window], axis=0))
    hi, lo = split(mixed)
    mixed = dot(jnp.concatenate([hi, lo, hi], axis=1), cols_w[...])
    (ar, ai), (br, bi) = butterfly(mixed, radius)
    core, quarter = place_ref[0], place_ref[1]
    for slot in range(8):
        half = core if slot < 4 else 1 - core
        f = 4 * half + (quarter ^ (slot % 4))
        pr, pi, mr, mi = spec_ref[f, 0], spec_ref[f, 1], spec_ref[f, 2], spec_ref[f, 3]
        plus = (pr * ar + pi * ai, pr * ai - pi * ar)
        minus = (mr * br + mi * bi, mr * bi - mi * br)
        value = inverse(plus, minus, rows_b[...], cols_b[...])
        if slot < 4:
            keep_ref[slot] = value
        else:
            send_ref[slot - 4] = value


def input_kernel(two, place_ref, spec_ref, filt_ref, rows_ref, cols_ref, rows_b, cols_b, *outs):
    count, radius = filt_ref.shape[0], filt_ref.shape[1]
    total = None
    for f in range(0, count, 2):
        spectra = near_spectra(filt_ref[f], filt_ref[f + 1], rows_ref[...], cols_ref[...], radius)
        for g, ((ar, ai), (br, bi)) in enumerate(spectra):
            pr, pi, mr, mi = (spec_ref[f + g, c] for c in range(4))
            term = (pr * ar - pi * ai, pr * ai + pi * ar, mr * br - mi * bi, mr * bi + mi * br)
            total = term if total is None else tuple(t + u for t, u in zip(total, term))
    full = inverse(total[:2], total[2:], rows_b[...], cols_b[...])
    own_ref, side_ref, below_ref, corner_ref = outs
    own_ref[...] = full[:radius, :radius]
    side_ref[...] = full[:radius, radius:]
    below, corner = full[radius:, :radius], full[radius:, radius:]
    if two:
        half = radius // 2
        first = place_ref[2] == 0
        below_ref[...] = jnp.where(first, below[:half], below[half:])
        corner_ref[...] = jnp.where(first, corner[:half], corner[half:])
    else:
        below_ref[...] = below
        corner_ref[...] = corner


def gather_kernel(place_ref, *refs):
    pieces, out_ref = refs[:8], refs[8]
    core, quarter = place_ref[0], place_ref[1]
    for slot in range(8):
        half = core if slot < 4 else 1 - core
        out_ref[4 * half + (quarter ^ (slot % 4))] = pieces[slot][...]


VMEM = pl.BlockSpec(memory_space=pltpu.VMEM)
SMEM = pl.BlockSpec(memory_space=pltpu.SMEM)
LIMIT = pltpu.CompilerParams(vmem_limit_bytes=32 * 1024 * 1024)


def local(table, across, along, retard, cotangent, filters):
    count, radius = filters.shape[0], filters.shape[1]
    two = across == 2
    block = jax.ShapeDtypeStruct((radius, radius), f32)
    row_index, col_index = lax.axis_index("across"), lax.axis_index("along")
    core = col_index & 1
    quarter = ((col_index >> 1) & 1) + 2 * (row_index & 1)
    place = jnp.stack([core, quarter, row_index]).astype(jnp.int32)

    def move(value, change):
        pairs = []
        for a in range(across):
            for b in range(along):
                c, d = change(a, b)
                if 0 <= c < across and 0 <= d < along:
                    pairs.append((a * along + b, c * along + d))
        return lax.ppermute(value, AXES, pairs)

    def around(side, below, corner):
        result = [move(side, lambda a, b: (a, b + 1)), move(side, lambda a, b: (a, b - 1))]
        if two:
            result.append(move(below, lambda a, b: (1 - a, b)))
            result.append(move(corner, lambda a, b: (1 - a, b + 1)))
            result.append(move(corner, lambda a, b: (1 - a, b - 1)))
        else:
            for s in (1, -1):
                result.append(move(below, lambda a, b: (a + s, b)))
                result.append(move(corner, lambda a, b: (a + s, b + 1)))
                result.append(move(corner, lambda a, b: (a + s, b - 1)))
        return result

    pieces = around(retard, retard, retard)
    spectra = pl.pallas_call(
        cotangent_kernel,
        out_shape=jax.ShapeDtypeStruct((count, 4, radius, radius), f32),
        in_specs=[VMEM] * 3,
        out_specs=VMEM,
        compiler_params=LIMIT,
        name="cotangent_spectra",
    )(cotangent, table["rows_near"], table["cols_near"])
    half = jax.ShapeDtypeStruct((count // 2, radius, radius), f32)
    keep, send = pl.pallas_call(
        functools.partial(filters_kernel, two),
        out_shape=(half, half),
        in_specs=[SMEM] + [VMEM] * (6 + len(pieces)),
        out_specs=(VMEM, VMEM),
        compiler_params=LIMIT,
        name="grad_filters",
    )(
        place,
        spectra,
        retard,
        *pieces,
        table["rows_wide"],
        table["cols_wide"],
        table["back_rows_near"],
        table["back_cols_near"],
    )
    strip = jax.ShapeDtypeStruct((radius // 2, radius), f32) if two else block
    own, side, below, corner = pl.pallas_call(
        functools.partial(input_kernel, two),
        out_shape=(block, block, strip, strip),
        in_specs=[SMEM] + [VMEM] * 6,
        out_specs=(VMEM,) * 4,
        compiler_params=LIMIT,
        name="grad_input",
    )(
        place,
        spectra,
        filters,
        table["rows_near"],
        table["cols_near"],
        table["back_rows_wide"],
        table["back_cols_wide"],
    )

    got = move(send, lambda a, b: (a, b ^ 1))
    mine = [keep[n] + got[n] for n in range(4)]
    flips = [lambda a, b, n=n: (a ^ (n >> 1), b ^ ((n & 1) << 1)) for n in range(4)]
    value = mine[0] + sum(move(mine[n], flips[n]) for n in range(1, 4))
    bits = [(0, 1 << s) for s in range(2, (along - 1).bit_length())]
    bits += [(1 << s, 0) for s in range(1, (across - 1).bit_length())]
    for start in range(0, len(bits), 2):
        group = bits[start : start + 2]
        masks = group + ([tuple(p ^ q for p, q in zip(*group))] if len(group) == 2 else [])
        value = value + sum(
            move(value, lambda a, b, m=m: (a ^ m[0], b ^ m[1])) for m in masks
        )
    parts = [value] + [move(value, flips[n]) for n in range(1, 4)]
    parts += [move(part, lambda a, b: (a, b ^ 1)) for part in parts]
    grad_filters = pl.pallas_call(
        gather_kernel,
        out_shape=jax.ShapeDtypeStruct((count, radius, radius), f32),
        in_specs=[SMEM] + [VMEM] * 8,
        out_specs=VMEM,
        compiler_params=LIMIT,
        name="gather_filters",
    )(place, *parts)

    low_row = lax.broadcasted_iota(jnp.int32, (radius, radius), 0) < radius // 2
    low_col = lax.broadcasted_iota(jnp.int32, (radius, radius), 1) < radius // 2
    got = around(side, below, corner)
    grad_input = own + jnp.where(low_col, got[0], got[1])
    if two:
        strip = got[2] + jnp.where(low_col[: radius // 2], got[3], got[4])
        strip = jnp.concatenate([strip, strip], axis=0)
        grad_input = grad_input + jnp.where(low_row == (row_index == 1), strip, 0.0)
    else:
        above = got[2] + jnp.where(low_col, got[3], got[4])
        under = got[5] + jnp.where(low_col, got[6], got[7])
        grad_input = grad_input + jnp.where(low_row, above, under)
    return grad_input, grad_filters


def solution(mesh):
    across, along = mesh.shape["across"], mesh.shape["along"]

    def whole(retard, cotangent, filters):
        table = {k: jnp.asarray(v) for k, v in tables(filters.shape[1]).items()}
        return jax.shard_map(
            functools.partial(local, table, across, along),
            mesh=mesh,
            in_specs=(P("across", "along"), P(None, "across", "along"), P()),
            out_specs=(P("across", "along"), P()),
            check_vma=False,
        )(retard, cotangent, filters)

    return whole
```

```python
import functools
import math

import jax
import jax.numpy as jnp
import numpy as np
from jax import lax
from jax.experimental import pallas as pl
from jax.experimental.pallas import tpu as pltpu
from jax.sharding import PartitionSpec as P

AXES = ("across", "along")
f32 = jnp.float32
bf16 = jnp.bfloat16


def halves(table):
    upper = table.astype(np.float32).astype(jnp.bfloat16)
    lower = (table - upper.astype(np.float64)).astype(np.float32).astype(jnp.bfloat16)
    return upper, lower


def tables(radius):
    period = 2 * radius
    freq = np.arange(radius)[:, None] + 0.5

    def turn(position):
        angle = 2.0 * math.pi / period * freq * position[None, :]
        return np.cos(angle), np.sin(angle)

    near = np.arange(radius)
    wide = (np.arange(period) + radius // 2) % period
    out = {}
    cos_n, sin_n = turn(near)
    cos_w, sin_w = turn(wide)
    hi, lo = halves(np.concatenate([cos_n, sin_n], axis=0))
    out["rows_near"] = np.concatenate([hi, lo], axis=1)
    hi, lo = halves(np.concatenate([cos_n, -sin_n], axis=0).T)
    out["cols_near"] = np.concatenate([hi, hi, lo], axis=0)
    hi, lo = halves(np.concatenate([cos_w, sin_w], axis=0))
    out["rows_wide"] = np.concatenate([hi, lo], axis=1)
    hi, lo = halves(np.concatenate([cos_w, -sin_w], axis=0).T)
    out["cols_wide"] = np.concatenate([hi, hi, lo], axis=0)
    scale = 2.0 / period**2
    hi, lo = halves(np.concatenate([cos_n, sin_n], axis=0).T)
    out["back_rows_near"] = np.concatenate([hi, lo], axis=0)
    hi, lo = halves(np.concatenate([cos_n, -sin_n], axis=0) * scale)
    out["back_cols_near"] = np.concatenate([hi, lo], axis=1)
    hi, lo = halves(np.concatenate([cos_w, sin_w], axis=0).T)
    out["back_rows_wide"] = np.concatenate([hi, lo], axis=0)
    hi, lo = halves(np.concatenate([cos_w, -sin_w], axis=0) * scale)
    out["back_cols_wide"] = np.concatenate([hi, lo], axis=1)
    return out


def dot(a, b):
    return jnp.dot(a, b, preferred_element_type=f32)


def split(x):
    upper = x.astype(bf16)
    return upper, (x - upper.astype(f32)).astype(bf16)


def butterfly(mixed, radius):
    cr, ci = mixed[:radius, :radius], mixed[:radius, radius:]
    sr, si = mixed[radius:, :radius], mixed[radius:, radius:]
    return (cr + si, ci - sr), (cr - si, ci + sr)


def near_spectra(first, second, rows, cols, radius):
    pair = jnp.concatenate([first, second], axis=1)
    mixed = dot(rows, jnp.concatenate([pair, pair], axis=0))
    result = []
    for part in (mixed[:, :radius], mixed[:, radius:]):
        hi, lo = split(part)
        result.append(butterfly(dot(jnp.concatenate([hi, lo, hi], axis=1), cols), radius))
    return result


def inverse(plus, minus, rows, cols):
    (pr, pi), (mr, mi) = plus, minus
    mixed = jnp.concatenate(
        [
            jnp.concatenate([pr + mr, pi + mi], axis=1),
            jnp.concatenate([mi - pi, pr - mr], axis=1),
        ],
        axis=0,
    )
    count = rows.shape[0] // 2
    hi, lo = split(mixed)
    both = dot(rows, hi)
    part = both[:count] + both[count:] + dot(rows[:count], lo)
    width = cols.shape[1] // 2
    hi, lo = split(part)
    both = dot(hi, cols)
    return both[:, :width] + both[:, width:] + dot(lo, cols[:, :width])


def cotangent_kernel(cot_hbm, rows_hbm, cols_hbm, out_ref, cot_ref, rows_ref, cols_ref, sems):
    sources, targets = (cot_hbm, rows_hbm, cols_hbm), (cot_ref, rows_ref, cols_ref)
    copies = [
        pltpu.make_async_copy(source, target, sems.at[n])
        for n, (source, target) in enumerate(zip(sources, targets))
    ]
    for copy in copies:
        copy.start()
    for copy in copies:
        copy.wait()
    count, radius = cot_ref.shape[0], cot_ref.shape[1]
    for f in range(0, count, 2):
        spectra = near_spectra(cot_ref[f], cot_ref[f + 1], rows_ref[...], cols_ref[...], radius)
        for g, (plus, minus) in enumerate(spectra):
            out_ref[f + g, 0] = plus[0]
            out_ref[f + g, 1] = plus[1]
            out_ref[f + g, 2] = minus[0]
            out_ref[f + g, 3] = minus[1]


def window_of(own, pieces, place_ref):
    shape = own.shape
    row_edge, row_odd, col_edge, col_odd = (place_ref[n] for n in range(2, 6))
    low_row = lax.broadcasted_iota(jnp.int32, shape, 0) < shape[0] // 2
    low_col = lax.broadcasted_iota(jnp.int32, shape, 1) < shape[1] // 2
    zero = jnp.zeros(shape, f32)
    got = [p[...].astype(f32) for p in pieces]

    def pick(near, far, low, odd, edge):
        return jnp.where(low == (odd == 0), near, jnp.where(edge == 1, zero, far))

    side = pick(got[0], got[1], low_col, col_odd, col_edge)
    rows = []
    for n in range(2, len(got), 3):
        rows.append((got[n], pick(got[n + 1], got[n + 2], low_col, col_odd, col_edge)))
    if len(rows) == 1:
        rows.append((zero, zero))
    below, corner = (
        pick(near, far, low_row, row_odd, row_edge) for near, far in zip(rows[0], rows[1])
    )
    return jnp.concatenate(
        [
            jnp.concatenate([own, side.astype(bf16)], axis=1),
            jnp.concatenate([below.astype(bf16), corner.astype(bf16)], axis=1),
        ],
        axis=0,
    )


def filters_kernel(place_ref, spec_ref, own_ref, *rest):
    pieces, (rows_w, cols_w, rows_b, cols_b, keep_ref, send_ref) = rest[:-6], rest[-6:]
    radius = own_ref.shape[0]
    window = window_of(own_ref[...], pieces, place_ref)
    mixed = dot(rows_w[...], jnp.concatenate([window, window], axis=0))
    hi, lo = split(mixed)
    mixed = dot(jnp.concatenate([hi, lo, hi], axis=1), cols_w[...])
    (ar, ai), (br, bi) = butterfly(mixed, radius)
    core, quarter = place_ref[0], place_ref[1]
    for slot in range(8):
        half = core if slot < 4 else 1 - core
        f = 4 * half + (quarter ^ (slot % 4))
        pr, pi, mr, mi = spec_ref[f, 0], spec_ref[f, 1], spec_ref[f, 2], spec_ref[f, 3]
        plus = (pr * ar + pi * ai, pr * ai - pi * ar)
        minus = (mr * br + mi * bi, mr * bi - mi * br)
        value = inverse(plus, minus, rows_b[...], cols_b[...])
        if slot < 4:
            keep_ref[slot] = value
        else:
            send_ref[slot - 4] = value


def input_kernel(two, place_ref, spec_ref, filt_ref, rows_ref, cols_ref, rows_b, cols_b, own_ref, side_ref):
    count, radius = filt_ref.shape[0], filt_ref.shape[1]
    total = None
    for f in range(0, count, 2):
        spectra = near_spectra(filt_ref[f], filt_ref[f + 1], rows_ref[...], cols_ref[...], radius)
        for g, ((ar, ai), (br, bi)) in enumerate(spectra):
            pr, pi, mr, mi = (spec_ref[f + g, c] for c in range(4))
            term = (pr * ar - pi * ai, pr * ai + pi * ar, mr * br - mi * bi, mr * bi + mi * br)
            total = term if total is None else tuple(t + u for t, u in zip(total, term))
    full = inverse(total[:2], total[2:], rows_b[...], cols_b[...])
    if two:
        half = radius // 2
        far = jnp.where(place_ref[3] == 0, full[radius : radius + half], full[radius + half :])
        full = jnp.concatenate([full[:radius], far], axis=0)
    own_ref[...] = full[:, :radius]
    side_ref[...] = full[:, radius:]


def gather_kernel(place_ref, own_ref, *refs):
    pieces, strips, input_ref, out_ref = refs[:8], refs[8:-2], refs[-2], refs[-1]
    core, quarter, row_edge, row_odd = (place_ref[n] for n in range(4))
    for slot in range(8):
        half = core if slot < 4 else 1 - core
        out_ref[4 * half + (quarter ^ (slot % 4))] = pieces[slot][...]
    shape = own_ref.shape
    low_row = lax.broadcasted_iota(jnp.int32, shape, 0) < shape[0] // 2
    zero = jnp.zeros(shape, f32)
    if len(strips) == 1:
        strip = strips[0][...]
        near, far = jnp.concatenate([strip, strip], axis=0), zero
    else:
        near, far = strips[0][...], jnp.where(row_edge == 1, zero, strips[1][...])
    input_ref[...] = own_ref[...] + jnp.where(low_row == (row_odd == 1), near, far)


VMEM = pl.BlockSpec(memory_space=pltpu.VMEM)
HBM = pl.BlockSpec(memory_space=pltpu.HBM)
SMEM = pl.BlockSpec(memory_space=pltpu.SMEM)
LIMIT = pltpu.CompilerParams(vmem_limit_bytes=32 * 1024 * 1024)


def local(table, across, along, retard, cotangent, filters):
    count, radius = filters.shape[0], filters.shape[1]
    two = across == 2
    block = jax.ShapeDtypeStruct((radius, radius), f32)
    row_index, col_index = lax.axis_index("across"), lax.axis_index("along")
    place = jnp.stack(
        [
            col_index & 1,
            ((col_index >> 1) & 1) + 2 * (row_index & 1),
            ((row_index == 0) | (row_index == across - 1)).astype(jnp.int32),
            row_index & 1,
            ((col_index == 0) | (col_index == along - 1)).astype(jnp.int32),
            col_index & 1,
        ]
    ).astype(jnp.int32)

    def move(value, change):
        pairs = []
        for a in range(across):
            for b in range(along):
                c, d = change(a, b)
                pairs.append((a * along + b, c * along + d))
        return lax.ppermute(value, AXES, pairs)

    def near(index, size):
        return index ^ 1

    def far(index, size):
        other = ((index + 1) ^ 1) - 1
        return other if 0 <= other < size else index

    def stay(index, size):
        return index

    def to(row, col):
        return lambda a, b: (row(a, across), col(b, along))

    row_moves = (near,) if two else (near, far)
    pieces = [move(retard, to(stay, near)), move(retard, to(stay, far))]
    for row in row_moves:
        pieces += [move(retard, to(row, col)) for col in (stay, near, far)]
    spectra = pl.pallas_call(
        cotangent_kernel,
        out_shape=jax.ShapeDtypeStruct((count, 4, radius, radius), f32),
        in_specs=[HBM] * 3,
        out_specs=VMEM,
        scratch_shapes=[
            pltpu.VMEM(v.shape, bf16)
            for v in (cotangent, table["rows_near"], table["cols_near"])
        ]
        + [pltpu.SemaphoreType.DMA((3,))],
        compiler_params=LIMIT,
        name="cotangent_spectra",
    )(cotangent, table["rows_near"], table["cols_near"])
    half = jax.ShapeDtypeStruct((count // 2, radius, radius), f32)
    keep, send = pl.pallas_call(
        filters_kernel,
        out_shape=(half, half),
        in_specs=[SMEM] + [VMEM] * (6 + len(pieces)),
        out_specs=(VMEM, VMEM),
        compiler_params=LIMIT,
        name="grad_filters",
    )(
        place,
        spectra,
        retard,
        *pieces,
        table["rows_wide"],
        table["cols_wide"],
        table["back_rows_near"],
        table["back_cols_near"],
    )
    tall = jax.ShapeDtypeStruct((2 * radius - (radius // 2 if two else 0), radius), f32)
    own, side = pl.pallas_call(
        functools.partial(input_kernel, two),
        out_shape=(tall, tall),
        in_specs=[SMEM] + [VMEM] * 6,
        out_specs=(VMEM, VMEM),
        compiler_params=LIMIT,
        name="grad_input",
    )(
        place,
        spectra,
        filters,
        table["rows_near"],
        table["cols_near"],
        table["back_rows_wide"],
        table["back_cols_wide"],
    )

    got = move(send, lambda a, b: (a, b ^ 1))
    mine = [keep[n] + got[n] for n in range(4)]
    flips = [lambda a, b, n=n: (a ^ (n >> 1), b ^ ((n & 1) << 1)) for n in range(4)]
    value = mine[0] + sum(move(mine[n], flips[n]) for n in range(1, 4))
    bits = [(0, 1 << s) for s in range(2, (along - 1).bit_length())]
    bits += [(1 << s, 0) for s in range(1, (across - 1).bit_length())]
    for start in range(0, len(bits), 2):
        group = bits[start : start + 2]
        masks = group + ([tuple(p ^ q for p, q in zip(*group))] if len(group) == 2 else [])
        if start == 0:
            value, side = lax.optimization_barrier((value, side))
            beside = [move(side, to(stay, col)) for col in (near, far)]
        value = value + sum(
            move(value, lambda a, b, m=m: (a ^ m[0], b ^ m[1])) for m in masks
        )
    low_col = lax.broadcasted_iota(jnp.int32, tall.shape, 1) < radius // 2
    other = jnp.where((col_index == 0) | (col_index == along - 1), 0.0, beside[1])
    own = own + jnp.where(low_col == (col_index & 1 == 1), beside[0], other)
    strips = [move(own[radius:], to(row, stay)) for row in row_moves]
    parts = [value] + [move(value, flips[n]) for n in range(1, 4)]
    parts += [move(part, lambda a, b: (a, b ^ 1)) for part in parts]
    return pl.pallas_call(
        gather_kernel,
        out_shape=(block, jax.ShapeDtypeStruct((count, radius, radius), f32)),
        in_specs=[SMEM] + [VMEM] * (9 + len(strips)),
        out_specs=(VMEM, VMEM),
        compiler_params=LIMIT,
        name="gather_filters",
    )(place, own[:radius], *parts, *strips)


def solution(mesh):
    across, along = mesh.shape["across"], mesh.shape["along"]

    def whole(retard, cotangent, filters):
        table = {k: jnp.asarray(v) for k, v in tables(filters.shape[1]).items()}
        return jax.shard_map(
            functools.partial(local, table, across, along),
            mesh=mesh,
            in_specs=(P("across", "along"), P(None, "across", "along"), P()),
            out_specs=(P("across", "along"), P()),
            check_vma=False,
        )(retard, cotangent, filters)

    return whole
```

```python
import functools
import math

import jax
import jax.numpy as jnp
import numpy as np
from jax import lax
from jax.experimental import pallas as pl
from jax.experimental.pallas import tpu as pltpu
from jax.sharding import PartitionSpec as P

AXES = ("across", "along")
f32 = jnp.float32
bf16 = jnp.bfloat16


def halves(table):
    upper = table.astype(np.float32).astype(jnp.bfloat16)
    lower = (table - upper.astype(np.float64)).astype(np.float32).astype(jnp.bfloat16)
    return upper, lower


def tables(radius):
    period = 2 * radius
    freq = np.arange(radius)[:, None] + 0.5

    def turn(position):
        angle = 2.0 * math.pi / period * freq * position[None, :]
        return np.cos(angle), np.sin(angle)

    near = np.arange(radius)
    wide = (np.arange(period) + radius // 2) % period
    def stack(*parts):
        return np.concatenate(parts, axis=0)

    cos_n, sin_n = turn(near)
    cos_w, sin_w = turn(wide)
    scale = 2.0 / period**2
    rows_near = np.concatenate(halves(stack(cos_n, sin_n)), axis=1)
    hi, lo = halves(stack(cos_n, -sin_n).T)
    cols_near = stack(hi, hi, lo)
    rows_wide = stack(*halves(stack(cos_w, sin_w)))
    hi, lo = halves(stack(cos_w, -sin_w).T)
    cols_wide = stack(hi, hi, lo)
    back_rows_near = stack(*halves(stack(cos_n, sin_n).T))
    back_cols_near = np.concatenate(halves(stack(cos_n, -sin_n) * scale), axis=1)
    back_rows_wide = stack(*halves(stack(cos_w, sin_w).T))
    back_cols_wide = stack(*halves(stack(cos_w, -sin_w) * scale))
    return (
        stack(rows_near, cols_near),
        stack(rows_wide, cols_wide, back_rows_near, back_cols_near),
        stack(back_rows_wide, back_cols_wide),
    )


def dot(a, b):
    return jnp.dot(a, b, preferred_element_type=f32)


def split(x):
    upper = x.astype(bf16)
    return upper, (x - upper.astype(f32)).astype(bf16)


def butterfly(mixed, radius):
    cr, ci = mixed[:radius, :radius], mixed[:radius, radius:]
    sr, si = mixed[radius:, :radius], mixed[radius:, radius:]
    return (cr + si, ci - sr), (cr - si, ci + sr)


def near_spectra(first, second, table, radius):
    rows, cols = table[: 2 * radius], table[2 * radius :]
    pair = jnp.concatenate([first, second], axis=1)
    mixed = dot(rows, jnp.concatenate([pair, pair], axis=0))
    result = []
    for part in (mixed[:, :radius], mixed[:, radius:]):
        hi, lo = split(part)
        result.append(butterfly(dot(jnp.concatenate([hi, lo, hi], axis=1), cols), radius))
    return result


def mixed_back(plus, minus):
    (pr, pi), (mr, mi) = plus, minus
    return jnp.concatenate(
        [
            jnp.concatenate([pr + mr, pi + mi], axis=1),
            jnp.concatenate([mi - pi, pr - mr], axis=1),
        ],
        axis=0,
    )


def inverse_rows(mixed, rows):
    count = rows.shape[0] // 2
    hi, lo = split(mixed)
    both = dot(rows, hi)
    return both[:count] + both[count:] + dot(rows[:count], lo)


def inverse_near(plus, minus, rows, cols):
    part = inverse_rows(mixed_back(plus, minus), rows)
    width = cols.shape[1] // 2
    hi, lo = split(part)
    both = dot(hi, cols)
    return both[:, :width] + both[:, width:] + dot(lo, cols[:, :width])


def inverse_wide(plus, minus, rows, cols):
    part = inverse_rows(mixed_back(plus, minus), rows)
    hi, lo = split(part)
    upper, lower = cols[: cols.shape[0] // 2], cols[cols.shape[0] // 2 :]
    return dot(hi, upper) + dot(hi, lower) + dot(lo, upper)


def cotangent_kernel(cot_ref, table_ref, out_ref):
    count, radius = cot_ref.shape[0], cot_ref.shape[1]
    table = table_ref[...]
    for f in range(0, count, 2):
        spectra = near_spectra(cot_ref[f], cot_ref[f + 1], table, radius)
        for g, (plus, minus) in enumerate(spectra):
            out_ref[f + g, 0] = plus[0]
            out_ref[f + g, 1] = plus[1]
            out_ref[f + g, 2] = minus[0]
            out_ref[f + g, 3] = minus[1]


def window_of(own, pieces, place_ref):
    shape = own.shape
    row_edge, row_odd, col_edge, col_odd = (place_ref[n] for n in range(2, 6))
    low_row = lax.broadcasted_iota(jnp.int32, shape, 0) < shape[0] // 2
    low_col = lax.broadcasted_iota(jnp.int32, shape, 1) < shape[1] // 2
    zero = jnp.zeros(shape, f32)
    got = [p[...].astype(f32) for p in pieces]

    def pick(near, far, low, odd, edge):
        return jnp.where(low == (odd == 0), near, jnp.where(edge == 1, zero, far))

    side = pick(got[0], got[1], low_col, col_odd, col_edge)
    rows = []
    for n in range(2, len(got), 3):
        rows.append((got[n], pick(got[n + 1], got[n + 2], low_col, col_odd, col_edge)))
    if len(rows) == 1:
        rows.append((zero, zero))
    below, corner = (
        pick(near, far, low_row, row_odd, row_edge) for near, far in zip(rows[0], rows[1])
    )
    return jnp.concatenate(
        [
            jnp.concatenate([own, side.astype(bf16)], axis=1),
            jnp.concatenate([below.astype(bf16), corner.astype(bf16)], axis=1),
        ],
        axis=0,
    )


def filter_gradients(place_ref, spec_ref, window_spec, back_ref, base, away, out_ref):
    radius = window_spec[0].shape[0]
    ar, ai, br, bi = window_spec
    half, quarter = place_ref[0], place_ref[1]
    if away:
        half = 1 - half
    for slot in range(4):
        f = 4 * half + (quarter ^ slot)
        pr, pi, mr, mi = spec_ref[f, 0], spec_ref[f, 1], spec_ref[f, 2], spec_ref[f, 3]
        plus = (pr * ar + pi * ai, pr * ai - pi * ar)
        minus = (mr * br + mi * bi, mr * bi - mi * br)
        out_ref[slot] = inverse_near(
            plus,
            minus,
            back_ref[base : base + 2 * radius],
            back_ref[base + 2 * radius : base + 4 * radius],
        )


def send_kernel(place_ref, spec_ref, own_ref, *rest):
    pieces, (table_ref, out_ref, window_ref) = rest[:-3], rest[-3:]
    radius = own_ref.shape[0]
    side = 2 * radius
    window = window_of(own_ref[...], pieces, place_ref)
    mixed = dot(table_ref[:side], window) + dot(table_ref[side : 2 * side], window)
    hi, lo = split(mixed)
    mixed = dot(jnp.concatenate([hi, lo, hi], axis=1), table_ref[2 * side : 5 * side])
    plus, minus = butterfly(mixed, radius)
    for n, part in enumerate(plus + minus):
        window_ref[n] = part
    filter_gradients(place_ref, spec_ref, plus + minus, table_ref, 5 * side, True, out_ref)


def keep_kernel(place_ref, spec_ref, window_ref, table_ref, out_ref):
    side = table_ref.shape[1]
    spec = tuple(window_ref[n] for n in range(4))
    filter_gradients(place_ref, spec_ref, spec, table_ref, 5 * side, False, out_ref)


def input_kernel(two, place_ref, spec_ref, filt_ref, table_ref, back_ref, own_ref, side_ref):
    count, radius = filt_ref.shape[0], filt_ref.shape[1]
    table = table_ref[...]
    total = None
    for f in range(0, count, 2):
        spectra = near_spectra(filt_ref[f], filt_ref[f + 1], table, radius)
        for g, ((ar, ai), (br, bi)) in enumerate(spectra):
            pr, pi, mr, mi = (spec_ref[f + g, c] for c in range(4))
            term = (pr * ar - pi * ai, pr * ai + pi * ar, mr * br - mi * bi, mr * bi + mi * br)
            total = term if total is None else tuple(t + u for t, u in zip(total, term))
    full = inverse_wide(total[:2], total[2:], back_ref[: 4 * radius], back_ref[4 * radius :])
    if two:
        half = radius // 2
        far = jnp.where(place_ref[3] == 0, full[radius : radius + half], full[radius + half :])
        full = jnp.concatenate([full[:radius], far], axis=0)
    own_ref[...] = full[:, :radius]
    side_ref[...] = full[:, radius:]


def gather_kernel(place_ref, own_ref, *refs):
    pieces, strips, input_ref, out_ref = refs[:8], refs[8:-2], refs[-2], refs[-1]
    core, quarter, row_edge, row_odd = (place_ref[n] for n in range(4))
    for slot in range(8):
        half = core if slot < 4 else 1 - core
        out_ref[4 * half + (quarter ^ (slot % 4))] = pieces[slot][...]
    shape = own_ref.shape
    low_row = lax.broadcasted_iota(jnp.int32, shape, 0) < shape[0] // 2
    zero = jnp.zeros(shape, f32)
    if len(strips) == 1:
        strip = strips[0][...]
        near, far = jnp.concatenate([strip, strip], axis=0), zero
    else:
        near, far = strips[0][...], jnp.where(row_edge == 1, zero, strips[1][...])
    input_ref[...] = own_ref[...] + jnp.where(low_row == (row_odd == 1), near, far)


VMEM = pl.BlockSpec(memory_space=pltpu.VMEM)
SMEM = pl.BlockSpec(memory_space=pltpu.SMEM)
LIMIT = pltpu.CompilerParams(vmem_limit_bytes=12 * 1024 * 1024)


def local(table, across, along, retard, cotangent, filters):
    count, radius = filters.shape[0], filters.shape[1]
    two = across == 2
    row_index, col_index = lax.axis_index("across"), lax.axis_index("along")
    place = jnp.stack(
        [
            col_index & 1,
            ((col_index >> 1) & 1) + 2 * (row_index & 1),
            ((row_index == 0) | (row_index == across - 1)).astype(jnp.int32),
            row_index & 1,
            ((col_index == 0) | (col_index == along - 1)).astype(jnp.int32),
            col_index & 1,
        ]
    ).astype(jnp.int32)

    def move(value, change):
        pairs = []
        for a in range(across):
            for b in range(along):
                c, d = change(a, b)
                pairs.append((a * along + b, c * along + d))
        return lax.ppermute(value, AXES, pairs)

    def near(index, size):
        return index ^ 1

    def far(index, size):
        other = ((index + 1) ^ 1) - 1
        return other if 0 <= other < size else index

    def stay(index, size):
        return index

    def to(row, col):
        return lambda a, b: (row(a, across), col(b, along))

    row_moves = (near,) if two else (near, far)
    pieces = [move(retard, to(stay, near)), move(retard, to(stay, far))]
    for row in row_moves:
        pieces += [move(retard, to(row, col)) for col in (stay, near, far)]
    near_table, filter_table, input_table = table

    def call(kernel, outs, name, work, *operands):
        scalars = operands[0] is place
        return pl.pallas_call(
            kernel,
            out_shape=outs,
            in_specs=[SMEM] * scalars + [VMEM] * (len(operands) - scalars),
            out_specs=jax.tree.map(lambda _: VMEM, outs),
            compiler_params=LIMIT,
            cost_estimate=pl.CostEstimate(
                flops=work * radius**3,
                bytes_accessed=sum(v.size * v.dtype.itemsize for v in operands),
                transcendentals=0,
            ),
            name=name,
        )(*operands)

    def arrays(*shape):
        return jax.ShapeDtypeStruct(shape, f32)

    spectra = call(
        cotangent_kernel,
        arrays(count, 4, radius, radius),
        "cotangent_spectra",
        700,
        cotangent,
        near_table,
    )
    half = arrays(count // 2, radius, radius)
    send, window = call(
        send_kernel,
        (half, arrays(4, radius, radius)),
        "filters_send",
        1100,
        place,
        spectra,
        retard,
        *pieces,
        filter_table,
    )
    keep = call(keep_kernel, half, "filters_keep", 800, place, spectra, window, filter_table)
    tall = arrays(2 * radius - (radius // 2 if two else 0), radius)
    own, side = call(
        functools.partial(input_kernel, two),
        (tall, tall),
        "grad_input",
        1300,
        place,
        spectra,
        filters,
        near_table,
        input_table,
    )

    got = move(send, lambda a, b: (a, b ^ 1))
    mine = lax.optimization_barrier([keep[n] + got[n] for n in range(4)])
    flips = [lambda a, b, n=n: (a ^ (n >> 1), b ^ ((n & 1) << 1)) for n in range(4)]
    value = mine[0] + sum(move(mine[n], flips[n]) for n in range(1, 4))
    bits = [(0, 1 << s) for s in range(2, (along - 1).bit_length())]
    bits += [(1 << s, 0) for s in range(1, (across - 1).bit_length())]
    for start in range(0, len(bits), 2):
        group = bits[start : start + 2]
        masks = group + ([tuple(p ^ q for p, q in zip(*group))] if len(group) == 2 else [])
        if start == 0:
            value, side = lax.optimization_barrier((value, side))
            beside = [move(side, to(stay, col)) for col in (near, far)]
        value = value + sum(
            move(value, lambda a, b, m=m: (a ^ m[0], b ^ m[1])) for m in masks
        )
    low_col = lax.broadcasted_iota(jnp.int32, tall.shape, 1) < radius // 2
    other = jnp.where((col_index == 0) | (col_index == along - 1), 0.0, beside[1])
    own = own + jnp.where(low_col == (col_index & 1 == 1), beside[0], other)
    value, strip = lax.optimization_barrier((value, own[radius:]))
    strips = [move(strip, to(row, stay)) for row in row_moves]
    parts = [value] + [move(value, flips[n]) for n in range(1, 4)]
    parts[3], strips = lax.optimization_barrier((parts[3], strips))
    parts += [move(part, lambda a, b: (a, b ^ 1)) for part in parts]
    return call(
        gather_kernel,
        (arrays(radius, radius), arrays(count, radius, radius)),
        "gather_filters",
        0,
        place,
        own[:radius],
        *parts,
        *strips,
    )


def solution(mesh):
    across, along = mesh.shape["across"], mesh.shape["along"]

    def whole(retard, cotangent, filters):
        table = [jnp.asarray(v) for v in tables(filters.shape[1])]
        return jax.shard_map(
            functools.partial(local, table, across, along),
            mesh=mesh,
            in_specs=(P("across", "along"), P(None, "across", "along"), P()),
            out_specs=(P("across", "along"), P()),
            check_vma=False,
        )(retard, cotangent, filters)

    return whole
```

```python
import functools
import math

import jax
import jax.numpy as jnp
import numpy as np
from jax import lax
from jax.experimental import pallas as pl
from jax.experimental.pallas import tpu as pltpu
from jax.sharding import PartitionSpec as P

AXES = ("across", "along")
f32 = jnp.float32
bf16 = jnp.bfloat16


def halves(table):
    upper = table.astype(np.float32).astype(jnp.bfloat16)
    lower = (table - upper.astype(np.float64)).astype(np.float32).astype(jnp.bfloat16)
    return upper, lower


def tables(radius):
    period = 2 * radius
    freq = np.arange(radius)[:, None] + 0.5

    def turn(position):
        angle = 2.0 * math.pi / period * freq * position[None, :]
        return np.cos(angle), np.sin(angle)

    near = np.arange(radius)
    wide = (np.arange(period) + radius // 2) % period
    def stack(*parts):
        return np.concatenate(parts, axis=0)

    cos_n, sin_n = turn(near)
    cos_w, sin_w = turn(wide)
    scale = 2.0 / period**2
    rows_near = np.concatenate(halves(stack(cos_n, sin_n)), axis=1)
    hi, lo = halves(stack(cos_n, -sin_n).T)
    cols_near = stack(hi, hi, lo)
    rows_wide = stack(*halves(stack(cos_w, sin_w)))
    hi, lo = halves(stack(cos_w, -sin_w).T)
    cols_wide = stack(hi, hi, lo)
    back_rows_near = stack(*halves(stack(cos_n, sin_n).T))
    back_cols_near = np.concatenate(halves(stack(cos_n, -sin_n) * scale), axis=1)
    back_rows_wide = stack(*halves(stack(cos_w, sin_w).T))
    back_cols_wide = stack(*halves(stack(cos_w, -sin_w) * scale))
    return (
        stack(rows_near, cols_near),
        stack(rows_wide, cols_wide, back_rows_near, back_cols_near),
        stack(back_rows_wide, back_cols_wide),
    )


def dot(a, b):
    return jnp.dot(a, b, preferred_element_type=f32)


def split(x):
    upper = x.astype(bf16)
    return upper, (x - upper.astype(f32)).astype(bf16)


def butterfly(mixed, radius):
    cr, ci = mixed[:radius, :radius], mixed[:radius, radius:]
    sr, si = mixed[radius:, :radius], mixed[radius:, radius:]
    return (cr + si, ci - sr), (cr - si, ci + sr)


def near_spectra(first, second, table, radius):
    rows, cols = table[: 2 * radius], table[2 * radius :]
    pair = jnp.concatenate([first, second], axis=1)
    mixed = dot(rows, jnp.concatenate([pair, pair], axis=0))
    result = []
    for part in (mixed[:, :radius], mixed[:, radius:]):
        hi, lo = split(part)
        result.append(butterfly(dot(jnp.concatenate([hi, lo, hi], axis=1), cols), radius))
    return result


def mixed_back(plus, minus):
    (pr, pi), (mr, mi) = plus, minus
    return jnp.concatenate(
        [
            jnp.concatenate([pr + mr, pi + mi], axis=1),
            jnp.concatenate([mi - pi, pr - mr], axis=1),
        ],
        axis=0,
    )


def inverse_rows(mixed, rows):
    count = rows.shape[0] // 2
    hi, lo = split(mixed)
    both = dot(rows, hi)
    return both[:count] + both[count:] + dot(rows[:count], lo)


def inverse_wide(plus, minus, rows, cols):
    part = inverse_rows(mixed_back(plus, minus), rows)
    hi, lo = split(part)
    upper, lower = cols[: cols.shape[0] // 2], cols[cols.shape[0] // 2 :]
    return dot(hi, upper) + dot(hi, lower) + dot(lo, upper)


def cotangent_kernel(cot_ref, table_ref, out_ref):
    count, radius = cot_ref.shape[0], cot_ref.shape[1]
    table = table_ref[...]
    for f in range(0, count, 2):
        spectra = near_spectra(cot_ref[f], cot_ref[f + 1], table, radius)
        for g, (plus, minus) in enumerate(spectra):
            out_ref[f + g, 0] = plus[0]
            out_ref[f + g, 1] = plus[1]
            out_ref[f + g, 2] = minus[0]
            out_ref[f + g, 3] = minus[1]


def window_of(own, pieces, place_ref):
    shape = own.shape
    row_edge, row_odd, col_edge, col_odd = (place_ref[n] for n in range(2, 6))
    low_row = lax.broadcasted_iota(jnp.int32, shape, 0) < shape[0] // 2
    low_col = lax.broadcasted_iota(jnp.int32, shape, 1) < shape[1] // 2
    zero = jnp.zeros(shape, f32)
    got = [p[...].astype(f32) for p in pieces]

    def pick(near, far, low, odd, edge):
        return jnp.where(low == (odd == 0), near, jnp.where(edge == 1, zero, far))

    side = pick(got[-1], got[-2], low_col, col_odd, col_edge)
    rows = []
    for n in range(0, len(got) - 2, 3):
        rows.append((got[n], pick(got[n + 1], got[n + 2], low_col, col_odd, col_edge)))
    if len(rows) == 1:
        rows.append((zero, zero))
    below, corner = (
        pick(near, far, low_row, row_odd, row_edge) for near, far in zip(rows[0], rows[1])
    )
    return jnp.concatenate(
        [
            jnp.concatenate([own, side.astype(bf16)], axis=1),
            jnp.concatenate([below.astype(bf16), corner.astype(bf16)], axis=1),
        ],
        axis=0,
    )


def filter_gradients(place_ref, spec_ref, window_spec, back_ref, base, away, out_ref):
    radius = window_spec[0].shape[0]
    ar, ai, br, bi = window_spec
    half, quarter = place_ref[0], place_ref[1]
    if away:
        half = 1 - half
    rows = back_ref[base : base + 2 * radius]
    cols = back_ref[base + 2 * radius : base + 4 * radius]
    parts = []
    for slot in range(4):
        f = 4 * half + (quarter ^ slot)
        pr, pi, mr, mi = spec_ref[f, 0], spec_ref[f, 1], spec_ref[f, 2], spec_ref[f, 3]
        plus = (pr * ar + pi * ai, pr * ai - pi * ar)
        minus = (mr * br + mi * bi, mr * bi - mi * br)
        parts.append(split(inverse_rows(mixed_back(plus, minus), rows)))
    hi, lo = (jnp.concatenate(p, axis=0) for p in zip(*parts))
    both = dot(hi, cols)
    value = both[:, :radius] + both[:, radius:] + dot(lo, cols[:, :radius])
    for slot in range(4):
        out_ref[slot] = value[slot * radius : (slot + 1) * radius]


def send_kernel(place_ref, spec_ref, own_ref, *rest):
    pieces, (table_ref, out_ref, window_ref) = rest[:-3], rest[-3:]
    radius = own_ref.shape[0]
    side = 2 * radius
    window = window_of(own_ref[...], pieces, place_ref)
    mixed = dot(table_ref[:side], window) + dot(table_ref[side : 2 * side], window)
    hi, lo = split(mixed)
    mixed = dot(jnp.concatenate([hi, lo, hi], axis=1), table_ref[2 * side : 5 * side])
    plus, minus = butterfly(mixed, radius)
    for n, part in enumerate(plus + minus):
        window_ref[n] = part
    filter_gradients(place_ref, spec_ref, plus + minus, table_ref, 5 * side, True, out_ref)


def keep_kernel(place_ref, spec_ref, window_ref, table_ref, out_ref):
    side = table_ref.shape[1]
    spec = tuple(window_ref[n] for n in range(4))
    filter_gradients(place_ref, spec_ref, spec, table_ref, 5 * side, False, out_ref)


def input_kernel(two, place_ref, spec_ref, filt_ref, table_ref, back_ref, own_ref, side_ref):
    count, radius = filt_ref.shape[0], filt_ref.shape[1]
    table = table_ref[...]
    total = None
    for f in range(0, count, 2):
        spectra = near_spectra(filt_ref[f], filt_ref[f + 1], table, radius)
        for g, ((ar, ai), (br, bi)) in enumerate(spectra):
            pr, pi, mr, mi = (spec_ref[f + g, c] for c in range(4))
            term = (pr * ar - pi * ai, pr * ai + pi * ar, mr * br - mi * bi, mr * bi + mi * br)
            total = term if total is None else tuple(t + u for t, u in zip(total, term))
    full = inverse_wide(total[:2], total[2:], back_ref[: 4 * radius], back_ref[4 * radius :])
    if two:
        half = radius // 2
        far = jnp.where(place_ref[3] == 0, full[radius : radius + half], full[radius + half :])
        full = jnp.concatenate([full[:radius], far], axis=0)
    own_ref[...] = full[:, :radius]
    side_ref[...] = full[:, radius:]


def gather_kernel(place_ref, own_ref, *refs):
    pieces, strips, input_ref, out_ref = refs[:8], refs[8:-2], refs[-2], refs[-1]
    core, quarter, row_edge, row_odd = (place_ref[n] for n in range(4))
    for slot in range(8):
        half = core if slot < 4 else 1 - core
        out_ref[4 * half + (quarter ^ (slot % 4))] = pieces[slot][...]
    shape = own_ref.shape
    low_row = lax.broadcasted_iota(jnp.int32, shape, 0) < shape[0] // 2
    zero = jnp.zeros(shape, f32)
    if len(strips) == 1:
        strip = strips[0][...]
        near, far = jnp.concatenate([strip, strip], axis=0), zero
    else:
        near, far = strips[0][...], jnp.where(row_edge == 1, zero, strips[1][...])
    input_ref[...] = own_ref[...] + jnp.where(low_row == (row_odd == 1), near, far)


VMEM = pl.BlockSpec(memory_space=pltpu.VMEM)
SMEM = pl.BlockSpec(memory_space=pltpu.SMEM)
LIMIT = pltpu.CompilerParams(vmem_limit_bytes=12 * 1024 * 1024)


def local(table, across, along, retard, cotangent, filters):
    count, radius = filters.shape[0], filters.shape[1]
    two = across == 2
    row_index, col_index = lax.axis_index("across"), lax.axis_index("along")
    place = jnp.stack(
        [
            col_index & 1,
            ((col_index >> 1) & 1) + 2 * (row_index & 1),
            ((row_index == 0) | (row_index == across - 1)).astype(jnp.int32),
            row_index & 1,
            ((col_index == 0) | (col_index == along - 1)).astype(jnp.int32),
            col_index & 1,
        ]
    ).astype(jnp.int32)

    def move(value, change):
        pairs = []
        for a in range(across):
            for b in range(along):
                c, d = change(a, b)
                pairs.append((a * along + b, c * along + d))
        return lax.ppermute(value, AXES, pairs)

    def near(index, size):
        return index ^ 1

    def far(index, size):
        other = ((index + 1) ^ 1) - 1
        return other if 0 <= other < size else index

    def stay(index, size):
        return index

    def to(row, col):
        return lambda a, b: (row(a, across), col(b, along))

    row_moves = (near,) if two else (near, far)
    corners = [[move(retard, to(row, col)) for col in (near, far)] for row in row_moves]
    pieces = []
    for corner in corners:
        pieces += [move(corner[0], to(stay, near)), *corner]
    pieces += [move(retard, to(stay, col)) for col in (far, near)]
    near_table, filter_table, input_table = table

    def call(kernel, outs, name, work, *operands):
        scalars = operands[0] is place
        return pl.pallas_call(
            kernel,
            out_shape=outs,
            in_specs=[SMEM] * scalars + [VMEM] * (len(operands) - scalars),
            out_specs=jax.tree.map(lambda _: VMEM, outs),
            compiler_params=LIMIT,
            cost_estimate=pl.CostEstimate(
                flops=work * radius**3,
                bytes_accessed=sum(v.size * v.dtype.itemsize for v in operands),
                transcendentals=0,
            ),
            name=name,
        )(*operands)

    def arrays(*shape):
        return jax.ShapeDtypeStruct(shape, f32)

    spectra = call(
        cotangent_kernel,
        arrays(count, 4, radius, radius),
        "cotangent_spectra",
        700,
        cotangent,
        near_table,
    )
    half = arrays(count // 2, radius, radius)
    send, window = call(
        send_kernel,
        (half, arrays(4, radius, radius)),
        "filters_send",
        1100,
        place,
        spectra,
        retard,
        *pieces,
        filter_table,
    )
    keep = call(keep_kernel, half, "filters_keep", 800, place, spectra, window, filter_table)
    tall = arrays(2 * radius - (radius // 2 if two else 0), radius)
    own, side = call(
        functools.partial(input_kernel, two),
        (tall, tall),
        "grad_input",
        1300,
        place,
        spectra,
        filters,
        near_table,
        input_table,
    )

    got = move(send, lambda a, b: (a, b ^ 1))
    mine = lax.optimization_barrier([keep[n] + got[n] for n in range(4)])
    flips = [lambda a, b, n=n: (a ^ (n >> 1), b ^ ((n & 1) << 1)) for n in range(4)]
    value = mine[0] + sum(move(mine[n], flips[n]) for n in range(1, 4))
    bits = [(0, 1 << s) for s in range(2, (along - 1).bit_length())]
    bits += [(1 << s, 0) for s in range(1, (across - 1).bit_length())]
    for start in range(0, len(bits), 2):
        group = bits[start : start + 2]
        masks = group + ([tuple(p ^ q for p, q in zip(*group))] if len(group) == 2 else [])
        if start == 0:
            value, side = lax.optimization_barrier((value, side))
            beside = [move(side, to(stay, col)) for col in (near, far)]
        value = value + sum(
            move(value, lambda a, b, m=m: (a ^ m[0], b ^ m[1])) for m in masks
        )
    low_col = lax.broadcasted_iota(jnp.int32, tall.shape, 1) < radius // 2
    other = jnp.where((col_index == 0) | (col_index == along - 1), 0.0, beside[1])
    own = own + jnp.where(low_col == (col_index & 1 == 1), beside[0], other)
    value, strip = lax.optimization_barrier((value, own[radius:]))
    strips = [move(strip, to(row, stay)) for row in row_moves]
    parts = [value] + [move(value, flips[n]) for n in range(1, 4)]
    parts[3], strips = lax.optimization_barrier((parts[3], strips))
    parts += [move(part, lambda a, b: (a, b ^ 1)) for part in parts]
    return call(
        gather_kernel,
        (arrays(radius, radius), arrays(count, radius, radius)),
        "gather_filters",
        0,
        place,
        own[:radius],
        *parts,
        *strips,
    )


def solution(mesh):
    across, along = mesh.shape["across"], mesh.shape["along"]

    def whole(retard, cotangent, filters):
        table = [jnp.asarray(v) for v in tables(filters.shape[1])]
        return jax.shard_map(
            functools.partial(local, table, across, along),
            mesh=mesh,
            in_specs=(P("across", "along"), P(None, "across", "along"), P()),
            out_specs=(P("across", "along"), P()),
            check_vma=False,
        )(retard, cotangent, filters)

    return whole
```

```python
import functools
import math

import jax
import jax.numpy as jnp
import numpy as np
from jax import lax
from jax.experimental import pallas as pl
from jax.experimental.pallas import tpu as pltpu
from jax.sharding import PartitionSpec as P

AXES = ("across", "along")
f32 = jnp.float32
bf16 = jnp.bfloat16


def halves(table):
    upper = table.astype(np.float32).astype(jnp.bfloat16)
    lower = (table - upper.astype(np.float64)).astype(np.float32).astype(jnp.bfloat16)
    return upper, lower


def tables(radius):
    period = 2 * radius
    freq = np.arange(radius)[:, None] + 0.5

    def turn(position):
        angle = 2.0 * math.pi / period * freq * position[None, :]
        return np.cos(angle), np.sin(angle)

    near = np.arange(radius)
    wide = (np.arange(period) + radius // 2) % period
    def stack(*parts):
        return np.concatenate(parts, axis=0)

    cos_n, sin_n = turn(near)
    cos_w, sin_w = turn(wide)
    scale = 2.0 / period**2
    rows_near = np.concatenate(halves(stack(cos_n, sin_n)), axis=1)
    hi, lo = halves(stack(cos_n, -sin_n).T)
    cols_near = stack(hi, hi, lo)
    rows_wide = stack(*halves(stack(cos_w, sin_w)))
    hi, lo = halves(stack(cos_w, -sin_w).T)
    cols_wide = stack(hi, hi, lo)
    back_rows_near = stack(*halves(stack(cos_n, sin_n).T))
    back_cols_near = np.concatenate(halves(stack(cos_n, -sin_n) * scale), axis=1)
    back_rows_wide = stack(*halves(stack(cos_w, sin_w).T))
    back_cols_wide = stack(*halves(stack(cos_w, -sin_w) * scale))
    return (
        stack(rows_near, cols_near),
        stack(rows_wide, cols_wide, back_rows_near, back_cols_near),
        stack(back_rows_wide, back_cols_wide),
    )


def dot(a, b):
    return jnp.dot(a, b, preferred_element_type=f32)


def split(x):
    upper = x.astype(bf16)
    return upper, (x - upper.astype(f32)).astype(bf16)


def butterfly(mixed, radius):
    cr, ci = mixed[:radius, :radius], mixed[:radius, radius:]
    sr, si = mixed[radius:, :radius], mixed[radius:, radius:]
    return (cr + si, ci - sr), (cr - si, ci + sr)


def near_spectra(first, second, table, radius):
    rows, cols = table[: 2 * radius], table[2 * radius :]
    pair = jnp.concatenate([first, second], axis=1)
    mixed = dot(rows, jnp.concatenate([pair, pair], axis=0))
    result = []
    for part in (mixed[:, :radius], mixed[:, radius:]):
        hi, lo = split(part)
        result.append(butterfly(dot(jnp.concatenate([hi, lo, hi], axis=1), cols), radius))
    return result


def mixed_back(plus, minus):
    (pr, pi), (mr, mi) = plus, minus
    return jnp.concatenate(
        [
            jnp.concatenate([pr + mr, pi + mi], axis=1),
            jnp.concatenate([mi - pi, pr - mr], axis=1),
        ],
        axis=0,
    )


def inverse_rows(mixed, rows):
    count = rows.shape[0] // 2
    hi, lo = split(mixed)
    both = dot(rows, hi)
    return both[:count] + both[count:] + dot(rows[:count], lo)


def inverse_wide(plus, minus, rows, cols):
    part = inverse_rows(mixed_back(plus, minus), rows)
    hi, lo = split(part)
    upper, lower = cols[: cols.shape[0] // 2], cols[cols.shape[0] // 2 :]
    return dot(hi, upper) + dot(hi, lower) + dot(lo, upper)


def cotangent_kernel(cot_ref, table_ref, out_ref):
    count, radius = cot_ref.shape[0], cot_ref.shape[1]
    table = table_ref[...]
    for f in range(0, count, 2):
        spectra = near_spectra(cot_ref[f], cot_ref[f + 1], table, radius)
        for g, (plus, minus) in enumerate(spectra):
            out_ref[f + g, 0] = plus[0]
            out_ref[f + g, 1] = plus[1]
            out_ref[f + g, 2] = minus[0]
            out_ref[f + g, 3] = minus[1]


def window_of(own, pieces, place_ref):
    shape = own.shape
    row_edge, row_odd, col_edge, col_odd = (place_ref[n] for n in range(2, 6))
    low_row = lax.broadcasted_iota(jnp.int32, shape, 0) < shape[0] // 2
    low_col = lax.broadcasted_iota(jnp.int32, shape, 1) < shape[1] // 2
    zero = jnp.zeros(shape, f32)
    got = [p[...].astype(f32) for p in pieces]

    def pick(near, far, low, odd, edge):
        return jnp.where(low == (odd == 0), near, jnp.where(edge == 1, zero, far))

    side = pick(got[-1], got[-2], low_col, col_odd, col_edge)
    rows = []
    for n in range(0, len(got) - 2, 3):
        rows.append((got[n], pick(got[n + 1], got[n + 2], low_col, col_odd, col_edge)))
    if len(rows) == 1:
        rows.append((zero, zero))
    below, corner = (
        pick(near, far, low_row, row_odd, row_edge) for near, far in zip(rows[0], rows[1])
    )
    return jnp.concatenate(
        [
            jnp.concatenate([own, side.astype(bf16)], axis=1),
            jnp.concatenate([below.astype(bf16), corner.astype(bf16)], axis=1),
        ],
        axis=0,
    )


def filter_gradients(place_ref, spec_ref, window_spec, back_ref, base, away, out_ref):
    radius = window_spec[0].shape[0]
    ar, ai, br, bi = window_spec
    half, quarter = place_ref[0], place_ref[1]
    if away:
        half = 1 - half
    rows = back_ref[base : base + 2 * radius]
    cols = back_ref[base + 2 * radius : base + 4 * radius]
    parts = []
    for slot in range(4):
        f = 4 * half + (quarter ^ slot)
        pr, pi, mr, mi = spec_ref[f, 0], spec_ref[f, 1], spec_ref[f, 2], spec_ref[f, 3]
        plus = (pr * ar + pi * ai, pr * ai - pi * ar)
        minus = (mr * br + mi * bi, mr * bi - mi * br)
        parts.append(split(inverse_rows(mixed_back(plus, minus), rows)))
    hi, lo = (jnp.concatenate(p, axis=0) for p in zip(*parts))
    both = dot(hi, cols)
    value = both[:, :radius] + both[:, radius:] + dot(lo, cols[:, :radius])
    for slot in range(4):
        out_ref[slot] = value[slot * radius : (slot + 1) * radius]


def send_kernel(place_ref, spec_ref, own_ref, *rest):
    pieces, (table_ref, out_ref, window_ref) = rest[:-3], rest[-3:]
    radius = own_ref.shape[0]
    side = 2 * radius
    window = window_of(own_ref[...], pieces, place_ref)
    mixed = dot(table_ref[:side], window) + dot(table_ref[side : 2 * side], window)
    hi, lo = split(mixed)
    mixed = dot(jnp.concatenate([hi, lo, hi], axis=1), table_ref[2 * side : 5 * side])
    plus, minus = butterfly(mixed, radius)
    for n, part in enumerate(plus + minus):
        window_ref[n] = part
    filter_gradients(place_ref, spec_ref, plus + minus, table_ref, 5 * side, True, out_ref)


def keep_kernel(place_ref, spec_ref, window_ref, table_ref, out_ref):
    side = table_ref.shape[1]
    spec = tuple(window_ref[n] for n in range(4))
    filter_gradients(place_ref, spec_ref, spec, table_ref, 5 * side, False, out_ref)


def input_kernel(two, place_ref, spec_ref, filt_ref, table_ref, back_ref, own_ref, side_ref):
    count, radius = filt_ref.shape[0], filt_ref.shape[1]
    table = table_ref[...]
    total = None
    for f in range(0, count, 2):
        spectra = near_spectra(filt_ref[f], filt_ref[f + 1], table, radius)
        for g, ((ar, ai), (br, bi)) in enumerate(spectra):
            pr, pi, mr, mi = (spec_ref[f + g, c] for c in range(4))
            term = (pr * ar - pi * ai, pr * ai + pi * ar, mr * br - mi * bi, mr * bi + mi * br)
            total = term if total is None else tuple(t + u for t, u in zip(total, term))
    full = inverse_wide(total[:2], total[2:], back_ref[: 4 * radius], back_ref[4 * radius :])
    if two:
        half = radius // 2
        far = jnp.where(place_ref[3] == 0, full[radius : radius + half], full[radius + half :])
        full = jnp.concatenate([full[:radius], far], axis=0)
    own_ref[...] = full[:, :radius]
    side_ref[...] = full[:, radius:]


VMEM = pl.BlockSpec(memory_space=pltpu.VMEM)
SMEM = pl.BlockSpec(memory_space=pltpu.SMEM)
LIMIT = pltpu.CompilerParams(vmem_limit_bytes=12 * 1024 * 1024)


def local(table, across, along, retard, cotangent, filters):
    count, radius = filters.shape[0], filters.shape[1]
    two = across == 2
    row_index, col_index = lax.axis_index("across"), lax.axis_index("along")
    place = jnp.stack(
        [
            col_index & 1,
            ((col_index >> 1) & 1) + 2 * (row_index & 1),
            ((row_index == 0) | (row_index == across - 1)).astype(jnp.int32),
            row_index & 1,
            ((col_index == 0) | (col_index == along - 1)).astype(jnp.int32),
            col_index & 1,
        ]
    ).astype(jnp.int32)

    def move(value, change):
        pairs = []
        for a in range(across):
            for b in range(along):
                c, d = change(a, b)
                pairs.append((a * along + b, c * along + d))
        return lax.ppermute(value, AXES, pairs)

    def near(index, size):
        return index ^ 1

    def far(index, size):
        other = ((index + 1) ^ 1) - 1
        return other if 0 <= other < size else index

    def stay(index, size):
        return index

    def to(row, col):
        return lambda a, b: (row(a, across), col(b, along))

    row_moves = (near,) if two else (near, far)
    corners = [[move(retard, to(row, col)) for col in (near, far)] for row in row_moves]
    pieces = []
    for corner in corners:
        pieces += [move(corner[0], to(stay, near)), *corner]
    pieces += [move(retard, to(stay, col)) for col in (far, near)]
    near_table, filter_table, input_table = table

    def call(kernel, outs, name, work, *operands):
        scalars = operands[0] is place
        return pl.pallas_call(
            kernel,
            out_shape=outs,
            in_specs=[SMEM] * scalars + [VMEM] * (len(operands) - scalars),
            out_specs=jax.tree.map(lambda _: VMEM, outs),
            compiler_params=LIMIT,
            cost_estimate=pl.CostEstimate(
                flops=work * radius**3,
                bytes_accessed=sum(v.size * v.dtype.itemsize for v in operands),
                transcendentals=0,
            ),
            name=name,
        )(*operands)

    def arrays(*shape):
        return jax.ShapeDtypeStruct(shape, f32)

    spectra = call(
        cotangent_kernel,
        arrays(count, 4, radius, radius),
        "cotangent_spectra",
        700,
        cotangent,
        near_table,
    )
    half = arrays(count // 2, radius, radius)
    send, window = call(
        send_kernel,
        (half, arrays(4, radius, radius)),
        "filters_send",
        1100,
        place,
        spectra,
        retard,
        *pieces,
        filter_table,
    )
    keep = call(keep_kernel, half, "filters_keep", 800, place, spectra, window, filter_table)
    tall = arrays(2 * radius - (radius // 2 if two else 0), radius)
    own, side = call(
        functools.partial(input_kernel, two),
        (tall, tall),
        "grad_input",
        1300,
        place,
        spectra,
        filters,
        near_table,
        input_table,
    )

    got = move(send, lambda a, b: (a, b ^ 1))
    mine = lax.optimization_barrier([keep[n] + got[n] for n in range(4)])
    flips = [lambda a, b, n=n: (a ^ (n >> 1), b ^ ((n & 1) << 1)) for n in range(4)]
    value = mine[0] + sum(move(mine[n], flips[n]) for n in (3, 2, 1))
    bits = [(0, 1 << s) for s in range(2, (along - 1).bit_length())]
    bits += [(1 << s, 0) for s in range(1, (across - 1).bit_length())]
    for start in range(0, len(bits), 2):
        group = bits[start : start + 2]
        masks = group + ([tuple(p ^ q for p, q in zip(*group))] if len(group) == 2 else [])
        if start == 0:
            value, side = lax.optimization_barrier((value, side))
            beside = [move(side, to(stay, col)) for col in (near, far)]
        value = value + sum(
            move(value, lambda a, b, m=m: (a ^ m[0], b ^ m[1])) for m in masks[::-1]
        )
    low_col = lax.broadcasted_iota(jnp.int32, tall.shape, 1) < radius // 2
    other = jnp.where((col_index == 0) | (col_index == along - 1), 0.0, beside[1])
    own = own + jnp.where(low_col == (col_index & 1 == 1), beside[0], other)
    strips = [move(own[radius:], to(row, stay)) for row in row_moves]
    parts = [value] + [move(value, flips[n]) for n in range(1, 4)]
    parts += [move(part, lambda a, b: (a, b ^ 1)) for part in parts]
    for bit, flag in enumerate((col_index >> 1, row_index, col_index)):
        swap = flag & 1 == 1
        parts = [jnp.where(swap, parts[n ^ (1 << bit)], parts[n]) for n in range(8)]
    grad_filters = jnp.stack(parts)
    low_row = lax.broadcasted_iota(jnp.int32, (radius, radius), 0) < radius // 2
    near_strip = jnp.concatenate([strips[0]] * 2, axis=0) if two else strips[0]
    far_strip = 0.0
    if not two:
        far_strip = jnp.where((row_index == 0) | (row_index == across - 1), 0.0, strips[1])
    grad_input = own[:radius] + jnp.where(low_row == (row_index & 1 == 1), near_strip, far_strip)
    return grad_input, grad_filters


def solution(mesh):
    across, along = mesh.shape["across"], mesh.shape["along"]

    def whole(retard, cotangent, filters):
        table = [jnp.asarray(v) for v in tables(filters.shape[1])]
        return jax.shard_map(
            functools.partial(local, table, across, along),
            mesh=mesh,
            in_specs=(P("across", "along"), P(None, "across", "along"), P()),
            out_specs=(P("across", "along"), P()),
            check_vma=False,
        )(retard, cotangent, filters)

    return whole
```

```python
import functools
import math

import jax
import jax.numpy as jnp
import numpy as np
from jax import lax
from jax.experimental import pallas as pl
from jax.experimental.pallas import tpu as pltpu
from jax.sharding import PartitionSpec as P

AXES = ("across", "along")
f32 = jnp.float32
bf16 = jnp.bfloat16


def halves(table):
    upper = table.astype(np.float32).astype(jnp.bfloat16)
    lower = (table - upper.astype(np.float64)).astype(np.float32).astype(jnp.bfloat16)
    return upper, lower


def tables(radius):
    period = 2 * radius
    freq = np.arange(radius)[:, None] + 0.5

    def turn(position):
        angle = 2.0 * math.pi / period * freq * position[None, :]
        return np.cos(angle), np.sin(angle)

    near = np.arange(radius)
    wide = (np.arange(period) + radius // 2) % period
    def stack(*parts):
        return np.concatenate(parts, axis=0)

    cos_n, sin_n = turn(near)
    cos_w, sin_w = turn(wide)
    scale = 2.0 / period**2
    rows_wide = stack(*halves(stack(cos_w, sin_w)))
    hi, lo = halves(stack(cos_w, -sin_w).T)
    cols_wide = stack(hi, hi, lo)
    back_rows_near = stack(*halves(stack(cos_n, sin_n).T))
    back_cols_near = np.concatenate(halves(stack(cos_n, -sin_n) * scale), axis=1)
    back_rows_wide = stack(*halves(stack(cos_w, sin_w).T))
    back_cols_wide = stack(*halves(stack(cos_w, -sin_w) * scale))
    return (
        stack(rows_wide, cols_wide, back_rows_near, back_cols_near),
        stack(back_rows_wide, back_cols_wide),
    )


def dot(a, b):
    return jnp.dot(a, b, preferred_element_type=f32)


def split(x):
    upper = x.astype(bf16)
    return upper, (x - upper.astype(f32)).astype(bf16)


def butterfly(mixed, radius):
    cr, ci = mixed[:radius, :radius], mixed[:radius, radius:]
    sr, si = mixed[radius:, :radius], mixed[radius:, radius:]
    return (cr + si, ci - sr), (cr - si, ci + sr)


def near_spectra(first, second, table, radius):
    rows, cols = table[: 2 * radius], table[2 * radius :]
    pair = jnp.concatenate([first, second], axis=1)
    mixed = dot(rows, jnp.concatenate([pair, pair], axis=0))
    result = []
    for part in (mixed[:, :radius], mixed[:, radius:]):
        hi, lo = split(part)
        result.append(butterfly(dot(jnp.concatenate([hi, lo, hi], axis=1), cols), radius))
    return result


def mixed_back(plus, minus):
    (pr, pi), (mr, mi) = plus, minus
    return jnp.concatenate(
        [
            jnp.concatenate([pr + mr, pi + mi], axis=1),
            jnp.concatenate([mi - pi, pr - mr], axis=1),
        ],
        axis=0,
    )


def inverse_rows(mixed, rows):
    count = rows.shape[0] // 2
    hi, lo = split(mixed)
    both = dot(rows, hi)
    return both[:count] + both[count:] + dot(rows[:count], lo)


def inverse_wide(plus, minus, rows, cols):
    part = inverse_rows(mixed_back(plus, minus), rows)
    hi, lo = split(part)
    upper, lower = cols[: cols.shape[0] // 2], cols[cols.shape[0] // 2 :]
    return dot(hi, upper) + dot(hi, lower) + dot(lo, upper)


def table_kernel(out_ref):
    radius = out_ref.shape[1] // 2
    shape = (radius, radius)
    first = lax.broadcasted_iota(jnp.int32, shape, 0)
    second = lax.broadcasted_iota(jnp.int32, shape, 1)

    def turn(freq, position):
        steps = lax.rem((2 * freq + 1) * position, 4 * radius) - 2 * radius
        half = steps.astype(f32) * (math.pi / (4 * radius))
        square = half * half
        cosine, sine = jnp.ones(shape, f32), jnp.ones(shape, f32)
        for n in range(7, 0, -1):
            cosine = 1.0 - cosine * square * (1.0 / (2 * n * (2 * n - 1)))
            sine = 1.0 - sine * square * (1.0 / (2 * n * (2 * n + 1)))
        sine = sine * half
        return 2.0 * sine * sine - 1.0, -2.0 * sine * cosine

    for n, part in enumerate(turn(first, second)):
        hi, lo = split(part)
        out_ref[n * radius : (n + 1) * radius, :radius] = hi
        out_ref[n * radius : (n + 1) * radius, radius:] = lo
    for n, part in enumerate(turn(second, first)):
        hi, lo = split(part if n == 0 else -part)
        for place, value in zip((2, 3, 4), (hi, hi, lo)):
            out_ref[place * radius : (place + 1) * radius, n * radius : (n + 1) * radius] = value


def cotangent_kernel(cot_ref, table_ref, out_ref):
    count, radius = cot_ref.shape[0], cot_ref.shape[1]
    table = table_ref[...]
    for f in range(0, count, 2):
        spectra = near_spectra(cot_ref[f], cot_ref[f + 1], table, radius)
        for g, (plus, minus) in enumerate(spectra):
            out_ref[f + g, 0] = plus[0]
            out_ref[f + g, 1] = plus[1]
            out_ref[f + g, 2] = minus[0]
            out_ref[f + g, 3] = minus[1]


def window_of(own, pieces, place_ref):
    shape = own.shape
    row_edge, row_odd, col_edge, col_odd = (place_ref[n] for n in range(2, 6))
    low_row = lax.broadcasted_iota(jnp.int32, shape, 0) < shape[0] // 2
    low_col = lax.broadcasted_iota(jnp.int32, shape, 1) < shape[1] // 2
    zero = jnp.zeros(shape, f32)
    got = [p[...].astype(f32) for p in pieces]

    def pick(near, far, low, odd, edge):
        return jnp.where(low == (odd == 0), near, jnp.where(edge == 1, zero, far))

    side = pick(got[-1], got[-2], low_col, col_odd, col_edge)
    rows = []
    for n in range(0, len(got) - 2, 3):
        rows.append((got[n], pick(got[n + 1], got[n + 2], low_col, col_odd, col_edge)))
    if len(rows) == 1:
        rows.append((zero, zero))
    below, corner = (
        pick(near, far, low_row, row_odd, row_edge) for near, far in zip(rows[0], rows[1])
    )
    return jnp.concatenate(
        [
            jnp.concatenate([own, side.astype(bf16)], axis=1),
            jnp.concatenate([below.astype(bf16), corner.astype(bf16)], axis=1),
        ],
        axis=0,
    )


def filter_gradients(place_ref, spec_ref, window_spec, back_ref, base, away, out_ref):
    radius = window_spec[0].shape[0]
    ar, ai, br, bi = window_spec
    half, quarter = place_ref[0], place_ref[1]
    if away:
        half = 1 - half
    rows = back_ref[base : base + 2 * radius]
    cols = back_ref[base + 2 * radius : base + 4 * radius]
    parts = []
    for slot in range(4):
        f = 4 * half + (quarter ^ slot)
        pr, pi, mr, mi = spec_ref[f, 0], spec_ref[f, 1], spec_ref[f, 2], spec_ref[f, 3]
        plus = (pr * ar + pi * ai, pr * ai - pi * ar)
        minus = (mr * br + mi * bi, mr * bi - mi * br)
        parts.append(split(inverse_rows(mixed_back(plus, minus), rows)))
    hi, lo = (jnp.concatenate(p, axis=0) for p in zip(*parts))
    both = dot(hi, cols)
    value = both[:, :radius] + both[:, radius:] + dot(lo, cols[:, :radius])
    for slot in range(4):
        out_ref[slot] = value[slot * radius : (slot + 1) * radius]


def send_kernel(place_ref, spec_ref, own_ref, *rest):
    pieces, (table_ref, out_ref, window_ref) = rest[:-3], rest[-3:]
    radius = own_ref.shape[0]
    side = 2 * radius
    window = window_of(own_ref[...], pieces[::-1], place_ref)
    mixed = dot(table_ref[:side], window) + dot(table_ref[side : 2 * side], window)
    hi, lo = split(mixed)
    mixed = dot(jnp.concatenate([hi, lo, hi], axis=1), table_ref[2 * side : 5 * side])
    plus, minus = butterfly(mixed, radius)
    for n, part in enumerate(plus + minus):
        window_ref[n] = part
    filter_gradients(place_ref, spec_ref, plus + minus, table_ref, 5 * side, True, out_ref)


def keep_kernel(place_ref, spec_ref, window_ref, table_ref, out_ref):
    side = table_ref.shape[1]
    spec = tuple(window_ref[n] for n in range(4))
    filter_gradients(place_ref, spec_ref, spec, table_ref, 5 * side, False, out_ref)


def input_kernel(two, place_ref, spec_ref, filt_ref, table_ref, back_ref, own_ref, side_ref):
    count, radius = filt_ref.shape[0], filt_ref.shape[1]
    table = table_ref[...]
    total = None
    for f in range(0, count, 2):
        spectra = near_spectra(filt_ref[f], filt_ref[f + 1], table, radius)
        for g, ((ar, ai), (br, bi)) in enumerate(spectra):
            pr, pi, mr, mi = (spec_ref[f + g, c] for c in range(4))
            term = (pr * ar - pi * ai, pr * ai + pi * ar, mr * br - mi * bi, mr * bi + mi * br)
            total = term if total is None else tuple(t + u for t, u in zip(total, term))
    full = inverse_wide(total[:2], total[2:], back_ref[: 4 * radius], back_ref[4 * radius :])
    if two:
        half = radius // 2
        far = jnp.where(place_ref[3] == 0, full[radius : radius + half], full[radius + half :])
        full = jnp.concatenate([full[:radius], far], axis=0)
    own_ref[...] = full[:, :radius]
    side_ref[...] = full[:, radius:]


VMEM = pl.BlockSpec(memory_space=pltpu.VMEM)
SMEM = pl.BlockSpec(memory_space=pltpu.SMEM)
LIMIT = pltpu.CompilerParams(vmem_limit_bytes=12 * 1024 * 1024)


def local(table, across, along, retard, cotangent, filters):
    count, radius = filters.shape[0], filters.shape[1]
    two = across == 2
    row_index, col_index = lax.axis_index("across"), lax.axis_index("along")
    place = jnp.stack(
        [
            col_index & 1,
            ((col_index >> 1) & 1) + 2 * (row_index & 1),
            ((row_index == 0) | (row_index == across - 1)).astype(jnp.int32),
            row_index & 1,
            ((col_index == 0) | (col_index == along - 1)).astype(jnp.int32),
            col_index & 1,
        ]
    ).astype(jnp.int32)

    def move(value, change):
        pairs = []
        for a in range(across):
            for b in range(along):
                c, d = change(a, b)
                pairs.append((a * along + b, c * along + d))
        return lax.ppermute(value, AXES, pairs)

    def near(index, size):
        return index ^ 1

    def far(index, size):
        other = ((index + 1) ^ 1) - 1
        return other if 0 <= other < size else index

    def stay(index, size):
        return index

    def to(row, col):
        return lambda a, b: (row(a, across), col(b, along))

    row_moves = (near,) if two else (near, far)
    corners = [[move(retard, to(row, col)) for col in (near, far)] for row in row_moves]
    pieces = []
    for corner in corners:
        pieces += [move(corner[0], to(stay, near)), *corner]
    pieces += [move(retard, to(stay, col)) for col in (far, near)]
    filter_table, input_table = table

    def call(kernel, outs, name, work, *operands):
        scalars = bool(operands) and operands[0] is place
        return pl.pallas_call(
            kernel,
            out_shape=outs,
            in_specs=[SMEM] * scalars + [VMEM] * (len(operands) - scalars),
            out_specs=jax.tree.map(lambda _: VMEM, outs),
            compiler_params=LIMIT,
            cost_estimate=pl.CostEstimate(
                flops=work * radius**3,
                bytes_accessed=sum(v.size * v.dtype.itemsize for v in operands),
                transcendentals=0,
            ),
            name=name,
        )(*operands)

    def arrays(*shape):
        return jax.ShapeDtypeStruct(shape, f32)

    near_table = call(
        table_kernel,
        jax.ShapeDtypeStruct((5 * radius, 2 * radius), bf16),
        "near_table",
        20,
    )
    spectra = call(
        cotangent_kernel,
        arrays(count, 4, radius, radius),
        "cotangent_spectra",
        700,
        cotangent,
        near_table,
    )
    half = arrays(count // 2, radius, radius)
    send, window = call(
        send_kernel,
        (half, arrays(4, radius, radius)),
        "filters_send",
        1100,
        place,
        spectra,
        retard,
        *pieces[::-1],
        filter_table,
    )
    keep = call(keep_kernel, half, "filters_keep", 800, place, spectra, window, filter_table)
    tall = arrays(2 * radius - (radius // 2 if two else 0), radius)
    own, side = call(
        functools.partial(input_kernel, two),
        (tall, tall),
        "grad_input",
        1300,
        place,
        spectra,
        filters,
        near_table,
        input_table,
    )

    got = move(send, lambda a, b: (a, b ^ 1))
    mine = lax.optimization_barrier([keep[n] + got[n] for n in range(4)])
    flips = [lambda a, b, n=n: (a ^ (n >> 1), b ^ ((n & 1) << 1)) for n in range(4)]
    value = mine[0] + sum(move(mine[n], flips[n]) for n in (3, 2, 1))
    bits = [(0, 1 << s) for s in range(2, (along - 1).bit_length())]
    bits += [(1 << s, 0) for s in range(1, (across - 1).bit_length())]
    for start in range(0, len(bits), 2):
        group = bits[start : start + 2]
        masks = group + ([tuple(p ^ q for p, q in zip(*group))] if len(group) == 2 else [])
        if start == 0:
            value, side = lax.optimization_barrier((value, side))
            beside = [move(side, to(stay, col)) for col in (near, far)]
        value = value + sum(
            move(value, lambda a, b, m=m: (a ^ m[0], b ^ m[1])) for m in masks
        )
    low_col = lax.broadcasted_iota(jnp.int32, tall.shape, 1) < radius // 2
    other = jnp.where((col_index == 0) | (col_index == along - 1), 0.0, beside[1])
    own = own + jnp.where(low_col == (col_index & 1 == 1), beside[0], other)
    strips = [move(own[radius:], to(row, stay)) for row in row_moves]
    parts = [value] + [move(value, flips[n]) for n in range(1, 4)]
    parts += [move(part, lambda a, b: (a, b ^ 1)) for part in parts]
    for bit, flag in enumerate((col_index >> 1, row_index, col_index)):
        stay = flag & 1 == 0
        parts = [jnp.where(stay, parts[n], parts[n ^ (1 << bit)]) for n in range(8)]
    grad_filters = jnp.stack(parts)
    low_row = lax.broadcasted_iota(jnp.int32, (radius, radius), 0) < radius // 2
    near_strip = jnp.concatenate([strips[0]] * 2, axis=0) if two else strips[0]
    far_strip = 0.0
    if not two:
        far_strip = jnp.where((row_index == 0) | (row_index == across - 1), 0.0, strips[1])
    grad_input = own[:radius] + jnp.where(low_row == (row_index & 1 == 1), near_strip, far_strip)
    return grad_input, grad_filters


def solution(mesh):
    across, along = mesh.shape["across"], mesh.shape["along"]

    def whole(retard, cotangent, filters):
        table = [jnp.asarray(v) for v in tables(filters.shape[1])]
        return jax.shard_map(
            functools.partial(local, table, across, along),
            mesh=mesh,
            in_specs=(P("across", "along"), P(None, "across", "along"), P()),
            out_specs=(P("across", "along"), P()),
            check_vma=False,
        )(retard, cotangent, filters)

    return whole
```

```python
import functools
import math

import jax
import jax.numpy as jnp
import numpy as np
from jax import lax
from jax.experimental import pallas as pl
from jax.experimental.pallas import tpu as pltpu
from jax.sharding import PartitionSpec as P

AXES = ("across", "along")
f32 = jnp.float32
bf16 = jnp.bfloat16


def halves(table):
    upper = table.astype(np.float32).astype(jnp.bfloat16)
    lower = (table - upper.astype(np.float64)).astype(np.float32).astype(jnp.bfloat16)
    return upper, lower


def tables(radius):
    period = 2 * radius
    freq = np.arange(radius)[:, None] + 0.5

    def turn(position):
        angle = 2.0 * math.pi / period * freq * position[None, :]
        return np.cos(angle), np.sin(angle)

    near = np.arange(radius)
    wide = (np.arange(period) + radius // 2) % period
    def stack(*parts):
        return np.concatenate(parts, axis=0)

    cos_n, sin_n = turn(near)
    cos_w, sin_w = turn(wide)
    scale = 2.0 / period**2
    rows_wide = stack(*halves(stack(cos_w, sin_w)))
    hi, lo = halves(stack(cos_w, -sin_w).T)
    cols_wide = stack(hi, hi, lo)
    back_rows_near = stack(*halves(stack(cos_n, sin_n).T))
    back_cols_near = np.concatenate(halves(stack(cos_n, -sin_n) * scale), axis=1)
    back_rows_wide = stack(*halves(stack(cos_w, sin_w).T))
    back_cols_wide = stack(*halves(stack(cos_w, -sin_w) * scale))
    return (
        stack(rows_wide, cols_wide, back_rows_near, back_cols_near),
        stack(back_rows_wide, back_cols_wide),
    )


def dot(a, b):
    return jnp.dot(a, b, preferred_element_type=f32)


def split(x):
    upper = x.astype(bf16)
    return upper, (x - upper.astype(f32)).astype(bf16)


def butterfly(mixed, radius):
    cr, ci = mixed[:radius, :radius], mixed[:radius, radius:]
    sr, si = mixed[radius:, :radius], mixed[radius:, radius:]
    return (cr + si, ci - sr), (cr - si, ci + sr)


def near_spectra(first, second, table, radius):
    rows, cols = table[: 2 * radius], table[2 * radius :]
    pair = jnp.concatenate([first, second], axis=1)
    mixed = dot(rows, jnp.concatenate([pair, pair], axis=0))
    result = []
    for part in (mixed[:, :radius], mixed[:, radius:]):
        hi, lo = split(part)
        result.append(butterfly(dot(jnp.concatenate([hi, lo, hi], axis=1), cols), radius))
    return result


def mixed_back(plus, minus):
    (pr, pi), (mr, mi) = plus, minus
    return jnp.concatenate(
        [
            jnp.concatenate([pr + mr, pi + mi], axis=1),
            jnp.concatenate([mi - pi, pr - mr], axis=1),
        ],
        axis=0,
    )


def inverse_rows(mixed, rows):
    count = rows.shape[0] // 2
    hi, lo = split(mixed)
    both = dot(rows, hi)
    return both[:count] + both[count:] + dot(rows[:count], lo)


def inverse_wide(plus, minus, rows, cols):
    part = inverse_rows(mixed_back(plus, minus), rows)
    hi, lo = split(part)
    upper, lower = cols[: cols.shape[0] // 2], cols[cols.shape[0] // 2 :]
    return dot(hi, upper) + dot(hi, lower) + dot(lo, upper)


def table_kernel(out_ref):
    radius = out_ref.shape[1] // 2
    shape = (radius, radius)
    first = lax.broadcasted_iota(jnp.int32, shape, 0)
    second = lax.broadcasted_iota(jnp.int32, shape, 1)

    def turn(freq, position):
        steps = lax.rem((2 * freq + 1) * position, 4 * radius) - 2 * radius
        half = steps.astype(f32) * (math.pi / (4 * radius))
        square = half * half
        cosine, sine = jnp.ones(shape, f32), jnp.ones(shape, f32)
        for n in range(7, 0, -1):
            cosine = 1.0 - cosine * square * (1.0 / (2 * n * (2 * n - 1)))
            sine = 1.0 - sine * square * (1.0 / (2 * n * (2 * n + 1)))
        sine = sine * half
        return 2.0 * sine * sine - 1.0, -2.0 * sine * cosine

    for n, part in enumerate(turn(first, second)):
        hi, lo = split(part)
        out_ref[n * radius : (n + 1) * radius, :radius] = hi
        out_ref[n * radius : (n + 1) * radius, radius:] = lo
    for n, part in enumerate(turn(second, first)):
        hi, lo = split(part if n == 0 else -part)
        for place, value in zip((2, 3, 4), (hi, hi, lo)):
            out_ref[place * radius : (place + 1) * radius, n * radius : (n + 1) * radius] = value


def cotangent_kernel(cot_ref, table_ref, out_ref):
    count, radius = cot_ref.shape[0], cot_ref.shape[1]
    table = table_ref[...]
    rows, cols = table[: 2 * radius], table[2 * radius :]
    parts = []
    for f in range(0, count, 2):
        pair = jnp.concatenate([cot_ref[f], cot_ref[f + 1]], axis=1)
        hi, lo = split(dot(rows, jnp.concatenate([pair, pair], axis=0)))
        for place in (slice(0, radius), slice(radius, 2 * radius)):
            parts.append(jnp.concatenate([hi[:, place], lo[:, place], hi[:, place]], axis=1))
    spectra = [butterfly(dot(part, cols), radius) for part in parts]
    for f, (plus, minus) in enumerate(spectra):
        out_ref[f, 0] = plus[0]
        out_ref[f, 1] = plus[1]
        out_ref[f, 2] = minus[0]
        out_ref[f, 3] = minus[1]


def window_of(own, pieces, place_ref):
    shape = own.shape
    row_edge, row_odd, col_edge, col_odd = (place_ref[n] for n in range(2, 6))
    low_row = lax.broadcasted_iota(jnp.int32, shape, 0) < shape[0] // 2
    low_col = lax.broadcasted_iota(jnp.int32, shape, 1) < shape[1] // 2
    zero = jnp.zeros(shape, f32)
    got = [p[...].astype(f32) for p in pieces]

    def pick(near, far, low, odd, edge):
        return jnp.where(low == (odd == 0), near, jnp.where(edge == 1, zero, far))

    side = pick(got[-1], got[-2], low_col, col_odd, col_edge)
    rows = []
    for n in range(0, len(got) - 2, 3):
        rows.append((got[n], pick(got[n + 1], got[n + 2], low_col, col_odd, col_edge)))
    if len(rows) == 1:
        rows.append((zero, zero))
    below, corner = (
        pick(near, far, low_row, row_odd, row_edge) for near, far in zip(rows[0], rows[1])
    )
    return jnp.concatenate(
        [
            jnp.concatenate([own, side.astype(bf16)], axis=1),
            jnp.concatenate([below.astype(bf16), corner.astype(bf16)], axis=1),
        ],
        axis=0,
    )


def filter_gradients(place_ref, spec_ref, window_spec, back_ref, base, away, out_ref):
    radius = window_spec[0].shape[0]
    ar, ai, br, bi = window_spec
    half, quarter = place_ref[0], place_ref[1]
    if away:
        half = 1 - half
    rows = back_ref[base : base + 2 * radius]
    cols = back_ref[base + 2 * radius : base + 4 * radius]
    parts = []
    for slot in range(4):
        f = 4 * half + (quarter ^ slot)
        pr, pi, mr, mi = spec_ref[f, 0], spec_ref[f, 1], spec_ref[f, 2], spec_ref[f, 3]
        plus = (pr * ar + pi * ai, pr * ai - pi * ar)
        minus = (mr * br + mi * bi, mr * bi - mi * br)
        parts.append(split(inverse_rows(mixed_back(plus, minus), rows)))
    hi, lo = (jnp.concatenate(p, axis=0) for p in zip(*parts))
    both = dot(hi, cols)
    value = both[:, :radius] + both[:, radius:] + dot(lo, cols[:, :radius])
    for slot in range(4):
        out_ref[slot] = value[slot * radius : (slot + 1) * radius]


def send_kernel(place_ref, spec_ref, own_ref, *rest):
    pieces, (table_ref, out_ref, window_ref) = rest[:-3], rest[-3:]
    radius = own_ref.shape[0]
    side = 2 * radius
    window = window_of(own_ref[...], pieces[::-1], place_ref)
    mixed = dot(table_ref[:side], window) + dot(table_ref[side : 2 * side], window)
    hi, lo = split(mixed)
    mixed = dot(jnp.concatenate([hi, lo, hi], axis=1), table_ref[2 * side : 5 * side])
    plus, minus = butterfly(mixed, radius)
    filter_gradients(place_ref, spec_ref, plus + minus, table_ref, 5 * side, True, out_ref)
    for n, part in enumerate(plus + minus):
        window_ref[n] = part


def keep_kernel(place_ref, spec_ref, window_ref, table_ref, out_ref):
    side = table_ref.shape[1]
    spec = tuple(window_ref[n] for n in range(4))
    filter_gradients(place_ref, spec_ref, spec, table_ref, 5 * side, False, out_ref)


def input_kernel(two, place_ref, spec_ref, filt_ref, table_ref, back_ref, own_ref, side_ref):
    count, radius = filt_ref.shape[0], filt_ref.shape[1]
    table = table_ref[...]
    total = None
    for f in range(0, count, 2):
        spectra = near_spectra(filt_ref[f], filt_ref[f + 1], table, radius)
        for g, ((ar, ai), (br, bi)) in enumerate(spectra):
            pr, pi, mr, mi = (spec_ref[f + g, c] for c in range(4))
            term = (pr * ar - pi * ai, pr * ai + pi * ar, mr * br - mi * bi, mr * bi + mi * br)
            total = term if total is None else tuple(t + u for t, u in zip(total, term))
    full = inverse_wide(total[:2], total[2:], back_ref[: 4 * radius], back_ref[4 * radius :])
    if two:
        half = radius // 2
        far = jnp.where(place_ref[3] == 0, full[radius : radius + half], full[radius + half :])
        full = jnp.concatenate([full[:radius], far], axis=0)
    own_ref[...] = full[:, :radius]
    side_ref[...] = full[:, radius:]


VMEM = pl.BlockSpec(memory_space=pltpu.VMEM)
SMEM = pl.BlockSpec(memory_space=pltpu.SMEM)
LIMIT = pltpu.CompilerParams(vmem_limit_bytes=12 * 1024 * 1024)


def local(table, across, along, retard, cotangent, filters):
    count, radius = filters.shape[0], filters.shape[1]
    two = across == 2
    row_index, col_index = lax.axis_index("across"), lax.axis_index("along")
    place = jnp.stack(
        [
            col_index & 1,
            ((col_index >> 1) & 1) + 2 * (row_index & 1),
            ((row_index == 0) | (row_index == across - 1)).astype(jnp.int32),
            row_index & 1,
            ((col_index == 0) | (col_index == along - 1)).astype(jnp.int32),
            col_index & 1,
        ]
    ).astype(jnp.int32)

    def move(value, change):
        pairs = []
        for a in range(across):
            for b in range(along):
                c, d = change(a, b)
                pairs.append((a * along + b, c * along + d))
        return lax.ppermute(value, AXES, pairs)

    def near(index, size):
        return index ^ 1

    def far(index, size):
        other = ((index + 1) ^ 1) - 1
        return other if 0 <= other < size else index

    def stay(index, size):
        return index

    def to(row, col):
        return lambda a, b: (row(a, across), col(b, along))

    row_moves = (near,) if two else (near, far)
    corners = [[move(retard, to(row, col)) for col in (near, far)] for row in row_moves]
    pieces = []
    for corner in corners:
        pieces += [move(corner[0], to(stay, near)), *corner]
    pieces += [move(retard, to(stay, col)) for col in (far, near)]
    filter_table, input_table = table

    def call(kernel, outs, name, work, *operands):
        scalars = bool(operands) and operands[0] is place
        return pl.pallas_call(
            kernel,
            out_shape=outs,
            in_specs=[SMEM] * scalars + [VMEM] * (len(operands) - scalars),
            out_specs=jax.tree.map(lambda _: VMEM, outs),
            compiler_params=LIMIT,
            cost_estimate=pl.CostEstimate(
                flops=work * radius**3,
                bytes_accessed=sum(v.size * v.dtype.itemsize for v in operands),
                transcendentals=0,
            ),
            name=name,
        )(*operands)

    def arrays(*shape):
        return jax.ShapeDtypeStruct(shape, f32)

    near_table = call(
        table_kernel,
        jax.ShapeDtypeStruct((5 * radius, 2 * radius), bf16),
        "near_table",
        20,
    )
    spectra = call(
        cotangent_kernel,
        arrays(count, 4, radius, radius),
        "cotangent_spectra",
        700,
        cotangent,
        near_table,
    )
    half = arrays(count // 2, radius, radius)
    send, window = call(
        send_kernel,
        (half, arrays(4, radius, radius)),
        "filters_send",
        1100,
        place,
        spectra,
        retard,
        *pieces[::-1],
        filter_table,
    )
    keep = call(keep_kernel, half, "filters_keep", 800, place, spectra, window, filter_table)
    tall = arrays(2 * radius - (radius // 2 if two else 0), radius)
    own, side = call(
        functools.partial(input_kernel, two),
        (tall, tall),
        "grad_input",
        1300,
        place,
        spectra,
        filters,
        near_table,
        input_table,
    )

    got = move(send, lambda a, b: (a, b ^ 1))
    mine = lax.optimization_barrier([keep[n] + got[n] for n in range(4)])
    flips = [lambda a, b, n=n: (a ^ (n >> 1), b ^ ((n & 1) << 1)) for n in range(4)]
    value = mine[0] + sum(move(mine[n], flips[n]) for n in (3, 2, 1))
    bits = [(0, 1 << s) for s in range(2, (along - 1).bit_length())]
    bits += [(1 << s, 0) for s in range(1, (across - 1).bit_length())]
    for start in range(0, len(bits), 2):
        group = bits[start : start + 2]
        masks = group + ([tuple(p ^ q for p, q in zip(*group))] if len(group) == 2 else [])
        if start == 0:
            value, side = lax.optimization_barrier((value, side))
            beside = [move(side, to(stay, col)) for col in (near, far)]
        value = value + sum(
            move(value, lambda a, b, m=m: (a ^ m[0], b ^ m[1])) for m in masks
        )
    low_col = lax.broadcasted_iota(jnp.int32, tall.shape, 1) < radius // 2
    other = jnp.where((col_index == 0) | (col_index == along - 1), 0.0, beside[1])
    own = own + jnp.where(low_col != (col_index & 1 == 1), other, beside[0])
    strips = [move(own[radius:], to(row, stay)) for row in row_moves]
    parts = [value] + [move(value, flips[n]) for n in range(1, 4)]
    parts += [move(part, lambda a, b: (a, b ^ 1)) for part in parts]
    for bit, flag in enumerate((col_index >> 1, row_index, col_index)):
        stay = flag & 1 == 0
        parts = [jnp.where(stay, parts[n], parts[n ^ (1 << bit)]) for n in range(8)]
    grad_filters = jnp.stack(parts)
    low_row = lax.broadcasted_iota(jnp.int32, (radius, radius), 0) < radius // 2
    near_strip = jnp.concatenate([strips[0]] * 2, axis=0) if two else strips[0]
    far_strip = 0.0
    if not two:
        far_strip = jnp.where((row_index == 0) | (row_index == across - 1), 0.0, strips[1])
    grad_input = own[:radius] + jnp.where(low_row == (row_index & 1 == 1), near_strip, far_strip)
    return grad_input, grad_filters


def solution(mesh):
    across, along = mesh.shape["across"], mesh.shape["along"]

    def whole(retard, cotangent, filters):
        table = [jnp.asarray(v) for v in tables(filters.shape[1])]
        return jax.shard_map(
            functools.partial(local, table, across, along),
            mesh=mesh,
            in_specs=(P("across", "along"), P(None, "across", "along"), P()),
            out_specs=(P("across", "along"), P()),
            check_vma=False,
        )(retard, cotangent, filters)

    return whole
```
